32 devices in a mesh: dp: 2 (over x), expert: 16 (over z, y, core).
Axes of the slice: x: 2, y: 2, z: 4, core: 2. Of those that a mesh axis runs over, the one named last changes fastest.
Arguments:
- tokens: bfloat16 [4096, 1024], P(('dp', 'expert')), may hold values from -6 to 6
- cotangent: bfloat16 [4096, 1024], P(('dp', 'expert')), may hold values from -4 to 4
- expert_ids: int32 [4096, 8], P(('dp', 'expert')), may hold values from 0 to 15, all different within a row; in each aligned block of 128 rows (0 to 127, 128 to 255, ...) at most 72 rows name the same one
- gate_probs: bfloat16 [4096, 8], P(('dp', 'expert')), may hold values from 0.049804688 to 0.29882812
- w_gate: bfloat16 [16, 1024, 384], P('expert'), may hold values from -0.1875 to 0.1875
- w_up: bfloat16 [16, 1024, 384], P('expert'), may hold values from -0.1875 to 0.1875
- w_down: bfloat16 [16, 384, 1024], P('expert'), may hold values from -0.3125 to 0.3125
Outputs:
- grad_tokens: bfloat16 [4096, 1024], P(('dp', 'expert'))
- grad_probs: bfloat16 [4096, 8], P(('dp', 'expert'))
- grad_w_gate: bfloat16 [16, 1024, 384], P('expert', 'dp')
- grad_w_up: bfloat16 [16, 1024, 384], P('expert', 'dp')
- grad_w_down: bfloat16 [16, 384, 1024], P('expert', 'dp')
The draws below stay inside these ranges and needn't reach their ends.
Inputs may be any that keep to these rules, and one draw needn't show every extreme that they name: `expert_ids`: each row names 8 different experts. Among the rows of one device no expert is named more than 72 times, and in some device's rows some expert is named exactly 72 times.
All inputs are finite; a program needn't handle non-finite values.
Results may differ from the reference program's by a relative error of at most 0.014.
Values may be sent and summed in bfloat16 or wider, within the bound.
No kernel may reach another device: no remote copies, remote signals or barrier semaphores. Data moves between devices by JAX's collectives and lax.ppermute only.
A program may use at most 64 MiB of HBM per device.

```python
import math
import jax
import jax.numpy as jnp
import numpy as np
from jax import lax

D = 1024
FF = 384
TOPK = 8
TOK_DEV = 128
EXPERTS = 16
MOST = 72
TOKENS = 4096
N_DP = 2
N_EXPERT = 16


def block_scale(key, extent, pieces, least, top_value):
    gain, own = 1.0, jax.random.fold_in(key, 6)
    for dim, shards_of in pieces:
        draws = jnp.exp(jax.random.uniform(jax.random.fold_in(own, dim), (shards_of,), jnp.float32, least / len(pieces), top_value / len(pieces)))
        gain = gain * jnp.repeat(draws, extent[dim] // shards_of).reshape([-1 if axis == dim else 1 for axis in range(len(extent))])
    return gain


def deal_out(own_key, own, number, rows, number_of, top, limit, lean):
    ranking = jax.random.permutation(own_key, number_of)
    crowded, common = load_shares(number_of, rows * top, limit, lean, True), load_shares(number_of, rows * top, limit, lean, False)
    places = jnp.arange(number_of)

    def named(lengths, offset_by):
        used = int((lengths > 0).sum())
        fixed = max(1, used // 4)
        moved = fixed + (places - fixed + offset_by * (used - fixed)) % max(1, number_of - fixed)
        return jnp.zeros((number_of,), jnp.int32).at[ranking[jnp.where(places < fixed, places, moved)]].set(jnp.asarray(lengths, jnp.int32))

    lengths = jnp.where(number % 4 == 0, named(crowded, number // 4), named(common, number - number // 4 - 1))
    mixed = jax.random.permutation(jax.random.fold_in(own, 3), number_of)
    donor, taker = mixed[0:number_of // 2 * 2:2], mixed[1:number_of // 2 * 2:2]
    margin = jnp.minimum(lengths[donor] - 1, limit - lengths[taker]) // 2
    margin = jnp.where((donor == ranking[0]) | (taker == ranking[0]) | (lengths[taker] == 0), 0, jnp.maximum(margin, 0))
    moved = jax.random.randint(jax.random.fold_in(own, 4), (number_of // 2,), 0, 1 << 20) % (margin + 1)
    lengths = lengths.at[donor].add(-moved).at[taker].add(moved)
    labels = jnp.searchsorted(jnp.cumsum(lengths), jnp.arange(rows * top), side="right").astype(jnp.int32)
    table = labels.reshape(top, rows).T
    table = table[jax.random.permutation(jax.random.fold_in(own, 1), rows)]
    offset_by = jax.random.randint(jax.random.fold_in(own, 2), (rows, 1), 0, top)
    return jnp.take_along_axis(table, (jnp.arange(top)[None, :] + offset_by) % top, axis=1)


def load_shares(amount, total, limit, lean, full):
    loads = [(1 << 20) // math.isqrt(rank ** lean) + 1 for rank in range(1, amount + 1)]
    largest = limit if full else min(limit, max(-(-total // amount), total * loads[0] // sum(loads)))
    least = 1 if total - largest >= amount - 1 else 0
    holding, spare = [largest] + [least] * (amount - 1), total - largest - least * (amount - 1)
    while spare > 0:
        free = [i for i in range(1, amount) if holding[i] < largest] or [i for i in range(1, amount) if holding[i] < limit]
        whole, budget = sum([loads[i] for i in free]), spare
        for i in free:
            addition = min(limit - holding[i], max(1, budget * loads[i] // whole), spare)
            holding[i] = holding[i] + addition
            spare = spare - addition
    return np.array(holding)


def centred(stream_key, extent, scale, most, split=(), kind=jnp.bfloat16):
    factor_of = block_scale(stream_key, extent, split, -0.22, 0.18) if split else 1.0
    drawn = jax.random.normal(stream_key, extent, jnp.float32) * scale * factor_of
    return jnp.minimum(jnp.maximum(drawn, -most), most).astype(kind)


def setup_inputs(seed: int = 0) -> dict:
    key_list = jax.random.split(jax.random.key(seed), 8)
    tokens = centred(key_list[0], (TOKENS, D), 1.0, 6.0, ((0, 32),))
    cotangent = centred(key_list[1], (TOKENS, D), 0.25, 4.0, ((0, 32),))
    expert_ids_keys = jax.random.split(jax.random.fold_in(key_list[2], 1), TOKENS // TOK_DEV)
    expert_ids_turns = jax.random.permutation(jax.random.fold_in(key_list[2], 3), TOKENS // TOK_DEV)
    expert_ids = jax.vmap(lambda own, number: deal_out(jax.random.fold_in(key_list[2], 2), own, number, TOK_DEV, EXPERTS, TOPK, MOST, 1))(expert_ids_keys, expert_ids_turns).reshape((TOKENS, TOPK))
    gate_probs = jnp.clip(0.049804688 + 0.24902344 * jax.random.uniform(key_list[3], (TOKENS, TOPK), jnp.float32) ** block_scale(key_list[3], (TOKENS, TOPK), ((0, 32),), -0.2, 0.2), 0.049804688, 0.29882812).astype(jnp.bfloat16)
    w_gate = centred(key_list[4], (EXPERTS, D, FF), D ** -0.5, 0.1875, ((0, 16),))
    w_up = centred(key_list[5], (EXPERTS, D, FF), D ** -0.5, 0.1875, ((0, 16),))
    w_down = centred(key_list[6], (EXPERTS, FF, D), FF ** -0.5, 0.3125, ((0, 16),))
    return dict(tokens=tokens, cotangent=cotangent, expert_ids=expert_ids, gate_probs=gate_probs, w_gate=w_gate, w_up=w_up, w_down=w_down)


def silu_parts(gate):
    sig = jax.nn.sigmoid(gate)
    return gate * sig, sig + gate * sig * (1.0 - sig)


def reference(tokens, cotangent, expert_ids, gate_probs, w_gate, w_up, w_down):
    blocks = TOKENS // TOK_DEV
    assigns = TOK_DEV * TOPK
    ids = expert_ids.reshape(blocks, assigns).astype(jnp.int32)
    onehot = (ids[:, :, None] == jnp.arange(EXPERTS, dtype=jnp.int32)[None, None, :]).astype(jnp.int32)
    ranks = jnp.cumsum(onehot, axis=1) - 1
    slots = jnp.sum(ranks * onehot, axis=2).astype(jnp.int32)
    target = ids * MOST + slots
    base = jnp.arange(blocks, dtype=jnp.int32)[:, None] * assigns
    filled = jnp.full((blocks, EXPERTS * MOST), -1, jnp.int32)
    filled = filled.at[jnp.arange(blocks, dtype=jnp.int32)[:, None], target].set(base + jnp.arange(assigns, dtype=jnp.int32)[None, :])
    empty_slot = filled < 0
    tok_index = jnp.where(empty_slot, TOKENS, filled // TOPK).astype(jnp.int32)
    prob_index = jnp.where(empty_slot, TOKENS * TOPK, filled).astype(jnp.int32)
    span = N_EXPERT * MOST
    tok_index = tok_index.reshape(N_DP, N_EXPERT, EXPERTS, MOST).transpose(2, 0, 1, 3).reshape(EXPERTS, N_DP, span)
    prob_index = prob_index.reshape(N_DP, N_EXPERT, EXPERTS, MOST).transpose(2, 0, 1, 3).reshape(EXPERTS, N_DP, span)
    zero_row = jnp.zeros((1, D), jnp.bfloat16)
    x_ext = jnp.concatenate([tokens, zero_row], axis=0)
    dy_ext = jnp.concatenate([cotangent, zero_row], axis=0)
    p_ext = jnp.concatenate([gate_probs.reshape(TOKENS * TOPK), jnp.zeros((1,), jnp.bfloat16)], axis=0)

    def one_expert(carry, inputs):
        grad_acc, prob_acc = carry
        rows_tok, rows_prob, weight_gate, weight_up, weight_down = inputs

        def one_group(inner, idx):
            acc, sums = inner
            tok_idx, p_idx = idx
            xr = x_ext[tok_idx]
            dyr = dy_ext[tok_idx]
            prob = p_ext[p_idx].astype(jnp.float32)[:, None]
            gate = jnp.dot(xr, weight_gate, preferred_element_type=jnp.float32)
            up = jnp.dot(xr, weight_up, preferred_element_type=jnp.float32)
            act, dact = silu_parts(gate)
            hidden = (act * up).astype(jnp.bfloat16)
            dz = jnp.dot(dyr, weight_down.T, preferred_element_type=jnp.float32)
            gp = jnp.sum(dz * hidden.astype(jnp.float32), axis=1).astype(jnp.bfloat16)
            dh = prob * dz
            d_gate = (dh * up * dact).astype(jnp.bfloat16)
            d_up = (dh * act).astype(jnp.bfloat16)
            scaled = (prob * dyr.astype(jnp.float32)).astype(jnp.bfloat16)
            row_grad = (jnp.dot(d_gate, weight_gate.T, preferred_element_type=jnp.float32)
                        + jnp.dot(d_up, weight_up.T, preferred_element_type=jnp.float32)).astype(jnp.bfloat16)
            part_gate = jnp.dot(xr.T, d_gate, preferred_element_type=jnp.float32).astype(jnp.bfloat16)
            part_up = jnp.dot(xr.T, d_up, preferred_element_type=jnp.float32).astype(jnp.bfloat16)
            part_down = jnp.dot(hidden.T, scaled, preferred_element_type=jnp.float32).astype(jnp.bfloat16)
            sums = (sums[0] + part_gate.astype(jnp.float32), sums[1] + part_up.astype(jnp.float32),
                    sums[2] + part_down.astype(jnp.float32))
            acc = (acc[0].at[tok_idx].add(row_grad.astype(jnp.float32)),
                   acc[1].at[p_idx].add(gp.astype(jnp.float32)))
            return (acc, sums), None

        init = ((grad_acc, prob_acc),
                (jnp.zeros((D, FF), jnp.float32), jnp.zeros((D, FF), jnp.float32), jnp.zeros((FF, D), jnp.float32)))
        (acc, sums), unused = lax.scan(one_group, init, (rows_tok, rows_prob))
        return acc, (sums[0].astype(jnp.bfloat16), sums[1].astype(jnp.bfloat16), sums[2].astype(jnp.bfloat16))

    start = (jnp.zeros((TOKENS + 1, D), jnp.float32), jnp.zeros((TOKENS * TOPK + 1,), jnp.float32))
    (grad_acc, prob_acc), (grad_gate, grad_up, grad_down) = lax.scan(
        one_expert, start, (tok_index, prob_index, w_gate, w_up, w_down))
    grad_tokens = grad_acc[:TOKENS].astype(jnp.bfloat16)
    grad_probs = prob_acc[:TOKENS * TOPK].reshape(TOKENS, TOPK).astype(jnp.bfloat16)
    return (grad_tokens, grad_probs, grad_gate, grad_up, grad_down)
```

```python
import functools

import jax
import jax.numpy as jnp
from jax import lax
from jax.experimental import pallas as pl
from jax.experimental.pallas import tpu as pltpu
from jax.sharding import PartitionSpec as P

BF16, F32 = jnp.bfloat16, jnp.float32
ROWS, LANES = 16, 128
VMEM = pl.BlockSpec(memory_space=pltpu.VMEM)
SMEM = pl.BlockSpec(memory_space=pltpu.SMEM)
PARAMS = pltpu.CompilerParams(vmem_limit_bytes=48 * 1024 * 1024)


def iota(shape, dim):
    return lax.broadcasted_iota(jnp.int32, shape, dim)


def nt(a, b):
    return lax.dot_general(a, b, (((1,), (1,)), ((), ())), preferred_element_type=F32)


def put_tiles(ref, first, value):
    rows, width = value.shape
    across = width // LANES
    for i in range(rows // ROWS):
        for j in range(across):
            ref[first + i * across + j] = value[
                i * ROWS : (i + 1) * ROWS, j * LANES : (j + 1) * LANES
            ]


def take_tiles(ref, first, dst, row, rows, width):
    across = width // LANES
    for i in range(rows // ROWS):
        for j in range(across):
            dst[row + i * ROWS : row + (i + 1) * ROWS, j * LANES : (j + 1) * LANES] = ref[
                first + i * across + j
            ]


def pack_kernel(tok_ref, cot_ref, ids_ref, prob_ref, a_ref, b_ref):
    tok_dev, width = tok_ref.shape
    half = tok_dev // 2
    block = half * width // (ROWS * LANES)
    ids, prob = ids_ref[...], prob_ref[...].astype(F32)
    for i in range(a_ref.shape[0] - 2 * block):
        expert = iota((ROWS, tok_dev), 0) + i * ROWS
        dense = jnp.zeros((ROWS, tok_dev), F32)
        for k in range(ids.shape[0]):
            dense += jnp.where(ids[k : k + 1] == expert, prob[k : k + 1], 0.0)
        a_ref[2 * block + i] = dense.astype(BF16)
        b_ref[2 * block + i] = dense.astype(BF16)
    for n, ref in enumerate((a_ref, b_ref)):
        put_tiles(ref, 0, tok_ref[n * half : (n + 1) * half])
        put_tiles(ref, block, cot_ref[n * half : (n + 1) * half])


def expert_kernel(
    me_ref,
    c0_ref,
    c1_ref,
    c2_ref,
    c3_ref,
    wg_ref,
    wu_ref,
    wd_ref,
    r0_ref,
    r1_ref,
    r2_ref,
    r3_ref,
    xt_ref,
    ht_ref,
    dgu_ref,
    sc_ref,
    x_ref,
    dy_ref,
):
    width, ff = wg_ref.shape
    chunks, grads = (c0_ref, c1_ref, c2_ref, c3_ref), (r0_ref, r1_ref, r2_ref, r3_ref)
    half = x_ref.shape[0] // 4
    block = half * width // (ROWS * LANES)
    me = me_ref[0]
    probs, eyes = [], []
    for n, ref in enumerate(chunks):
        take_tiles(ref, 0, x_ref, n * half, half, width)
        take_tiles(ref, block, dy_ref, n * half, half, width)
        row = jnp.zeros((1, LANES), F32)
        for i in range(ref.shape[0] - 2 * block):
            mine = iota((ROWS, LANES), 0) + i * ROWS == me
            row += jnp.sum(
                jnp.where(mine, ref[2 * block + i].astype(F32), 0.0), axis=0, keepdims=True
            )
        eye = iota((half, LANES), 0) + (n % 2) * half == iota((half, LANES), 1)
        probs.append(jnp.sum(jnp.where(eye, row, 0.0), axis=1, keepdims=True))
        eyes.append(eye)
    prob = jnp.concatenate(probs, axis=0)
    x, dy = x_ref[...], dy_ref[...]
    gate = jnp.dot(x, wg_ref[...], preferred_element_type=F32)
    up = jnp.dot(x, wu_ref[...], preferred_element_type=F32)
    dz = nt(dy, wd_ref[...])
    sig = jax.nn.sigmoid(gate)
    act, dact = gate * sig, sig + gate * sig * (1.0 - sig)
    hidden = (act * up).astype(BF16)
    gate_grad = jnp.sum(dz * hidden.astype(F32), axis=1, keepdims=True)
    dh = prob * dz
    d_gate = (dh * up * dact).astype(BF16)
    d_up = (dh * act).astype(BF16)
    rows = nt(d_gate, wg_ref[...]) + nt(d_up, wu_ref[...])
    for n, ref in enumerate(grads):
        put_tiles(ref, 0, rows[n * half : (n + 1) * half].astype(BF16))
        row = jnp.sum(
            jnp.where(eyes[n], gate_grad[n * half : (n + 1) * half], 0.0), axis=0, keepdims=True
        )
        for i in range(ref.shape[0] - block):
            mine = iota((ROWS, LANES), 0) + i * ROWS == me
            ref[block + i] = jnp.where(mine, row, 0.0).astype(BF16)
    dgu_ref[:, :ff] = d_gate
    dgu_ref[:, ff:] = d_up
    sc_ref[...] = (prob * dy.astype(F32)).astype(BF16)
    xt_ref[...] = x.T
    ht_ref[...] = hidden.T


def weight_kernel(groups, start, final, *refs):
    refs = refs[1:]
    in_w, in_d = (refs[:2]) if start else (None, None)
    refs = refs[2:] if start else refs
    total_w = in_w[...] if start else None
    total_d = in_d[...] if start else None
    for g in range(groups):
        xt, ht, dgu, sc = refs[4 * g : 4 * g + 4]
        w = jnp.dot(xt[...], dgu[...], preferred_element_type=F32)
        d = jnp.dot(ht[...], sc[...], preferred_element_type=F32)
        total_w = w if total_w is None else total_w + w
        total_d = d if total_d is None else total_d + d
    outs = refs[4 * groups :]
    if final:
        ff = outs[0].shape[1]
        outs[0][...] = total_w[:, :ff].astype(BF16)
        outs[1][...] = total_w[:, ff:].astype(BF16)
        outs[2][...] = total_d.astype(BF16)
    else:
        outs[0][...] = total_w
        outs[1][...] = total_d


def weight_sums(totals, groups, width, ff, part=None, parts=1, final=False):
    steps = 4 // parts
    tile_w, tile_d = width // 4, ff // 4
    first = jnp.zeros((1,), jnp.int32) if part is None else (part * steps).astype(jnp.int32)[None]
    row = lambda i, s: (s[0] + i, 0)
    whole = lambda i, s: (0, 0)
    out_row = lambda i, s: (i, 0)
    specs, args = [], []
    if totals is not None:
        specs += [pl.BlockSpec((tile_w, 2 * ff), row), pl.BlockSpec((tile_d, width), row)]
        args += list(totals)
    for xt, ht, dgu, sc in groups:
        k = xt.shape[1]
        specs += [
            pl.BlockSpec((tile_w, k), row),
            pl.BlockSpec((tile_d, k), row),
            pl.BlockSpec((k, 2 * ff), whole),
            pl.BlockSpec((k, width), whole),
        ]
        args += [xt, ht, dgu, sc]
    if final:
        blocks = ((tile_w, ff), (tile_w, ff), (tile_d, width))
        kind = BF16
    else:
        blocks = ((tile_w, 2 * ff), (tile_d, width))
        kind = F32
    rows = sum(g[0].shape[1] for g in groups)
    return pl.pallas_call(
        functools.partial(weight_kernel, len(groups), totals is not None, final),
        out_shape=tuple(jax.ShapeDtypeStruct((r * steps, c), kind) for r, c in blocks),
        grid_spec=pltpu.PrefetchScalarGridSpec(
            num_scalar_prefetch=1,
            grid=(steps,),
            in_specs=specs,
            out_specs=tuple(pl.BlockSpec(b, out_row) for b in blocks),
        ),
        compiler_params=PARAMS,
        cost_estimate=pl.CostEstimate(
            flops=6 * rows * width * ff // parts, bytes_accessed=8 * 2**20 // parts, transcendentals=0
        ),
        name="weight_sums",
    )(first, *args)


def home_kernel(count, ids_ref, *refs):
    out_ref, prob_ref = refs[2 * count :]
    tok_dev, width = out_ref.shape
    half = tok_dev // 2
    block = half * width // (ROWS * LANES)
    across = width // LANES
    sums = []
    for n in range(2):
        total = refs[n * count][...].astype(F32)
        for ref in refs[n * count + 1 : (n + 1) * count]:
            total += ref[...].astype(F32)
        for i in range(half // ROWS):
            for j in range(across):
                out_ref[
                    n * half + i * ROWS : n * half + (i + 1) * ROWS, j * LANES : (j + 1) * LANES
                ] = total[i * across + j].astype(BF16)
        sums.append(total[block:])
    by_expert = sums[0] + sums[1]
    ids = ids_ref[...]
    for k in range(ids.shape[0]):
        row = jnp.zeros((1, tok_dev), F32)
        for i in range(by_expert.shape[0]):
            expert = iota((ROWS, tok_dev), 0) + i * ROWS
            row += jnp.sum(
                jnp.where(ids[k : k + 1] == expert, by_expert[i], 0.0), axis=0, keepdims=True
            )
        prob_ref[k : k + 1] = row


def on_device(tokens, cotangent, expert_ids, gate_probs, w_gate, w_up, w_down):
    tok_dev, width = tokens.shape
    ff = w_gate.shape[2]
    half = tok_dev // 2
    devices = lax.axis_size("expert")
    groups = lax.axis_size("dp")
    experts = devices * w_gate.shape[0]
    block = half * width // (ROWS * LANES)
    extra = experts // ROWS

    chips = devices // 2
    ring = list(range(0, chips, 2)) + list(range(1, chips, 2))[::-1]
    hop = {
        d: [
            (2 * ring[i] + c, 2 * ring[(i + d) % chips] + c)
            for i in range(chips)
            for c in range(2)
        ]
        for d in (1, -1)
    }
    right = lambda v: lax.ppermute(v, "expert", hop[1])
    left = lambda v: lax.ppermute(v, "expert", hop[-1])
    swap = lambda v: lax.ppermute(v, "expert", [(i, i ^ 1) for i in range(devices)])
    full, odd = (chips - 1) // 2, chips % 2 == 0

    me = lax.axis_index("expert").astype(jnp.int32)[None]
    ids_t, probs_t = expert_ids.T, gate_probs.T
    wg, wu, wd = w_gate[0], w_up[0], w_down[0]

    chunk = jax.ShapeDtypeStruct((2 * block + extra, ROWS, LANES), BF16)
    a0, b0 = pl.pallas_call(
        pack_kernel,
        out_shape=(chunk, chunk),
        in_specs=[VMEM] * 4,
        out_specs=(VMEM, VMEM),
        compiler_params=PARAMS,
        name="pack",
    )(tokens, cotangent, ids_t, probs_t)

    grad = jax.ShapeDtypeStruct((block + extra, ROWS, LANES), BF16)

    def expert(first, second):
        rows = 4 * half
        outs = pl.pallas_call(
            expert_kernel,
            out_shape=(grad,) * 4
            + (
                jax.ShapeDtypeStruct((width, rows), BF16),
                jax.ShapeDtypeStruct((ff, rows), BF16),
                jax.ShapeDtypeStruct((rows, 2 * ff), BF16),
                jax.ShapeDtypeStruct((rows, width), BF16),
            ),
            in_specs=[SMEM] + [VMEM] * 7,
            out_specs=(VMEM,) * 8,
            scratch_shapes=[pltpu.VMEM((rows, width), BF16), pltpu.VMEM((rows, width), BF16)],
            compiler_params=PARAMS,
            cost_estimate=pl.CostEstimate(
                flops=10 * rows * width * ff, bytes_accessed=6 * 2**20, transcendentals=rows * ff
            ),
            name="expert",
        )(me, first, second, swap(first), swap(second), wg, wu, wd)
        mine = ((outs[0], swap(outs[2])), (outs[1], swap(outs[3])))
        return mine, outs[4:]

    home, group0 = expert(a0, b0)
    ra = la = a0
    rb = lb = b0
    local = {}
    group = {}
    for s in range(1, full + 1):
        ra, lb = right(ra), left(lb)
        (local["ra", s], local["lb", s]), group[s, 0] = expert(ra, lb)
        la, rb = left(la), right(rb)
        (local["la", s], local["rb", s]), group[s, 1] = expert(la, rb)
    if odd:
        ra, lb = right(ra), left(lb)
        (local["ra", full + 1], local["lb", full + 1]), group[full + 1, 0] = expert(ra, lb)

    order = [group0] + list(group.values())
    totals = None
    at = 0
    for n in range(0, len(order) - 2, 2):
        totals = weight_sums(totals, order[n : n + 2], width, ff)
        at = n + 2
    rest = order[at:]
    if groups == 2:
        here = lax.axis_index("dp")
        send = weight_sums(totals, rest, width, ff, 1 - here, 2, True)
        got = [lax.ppermute(v, "dp", [(0, 1), (1, 0)]) for v in send]
        keep = weight_sums(totals, rest, width, ff, here, 2, True)
        grads = [(a.astype(F32) + b.astype(F32)).astype(BF16) for a, b in zip(keep, got)]
    else:
        parts = weight_sums(totals, rest, width, ff, final=True)
        grads = [lax.psum_scatter(v, "dp", scatter_dimension=0, tiled=True) for v in parts]

    def add(*terms):
        return sum(t.astype(F32) for t in terms).astype(BF16)

    def back(name, first, move):
        moving = add(*local[name, first])
        for s in range(first - 1, 0, -1):
            moving = add(move(moving), *local[name, s])
        return move(moving)

    last = full + 1 if odd else full
    came_ra, came_lb = back("ra", last, left), back("lb", last, right)
    came_rb, came_la = back("rb", full, left), back("la", full, right)
    grad_tokens, grad_probs = pl.pallas_call(
        functools.partial(home_kernel, 4),
        out_shape=(
            jax.ShapeDtypeStruct((tok_dev, width), BF16),
            jax.ShapeDtypeStruct(ids_t.shape, F32),
        ),
        in_specs=[VMEM] * 9,
        out_specs=(VMEM, VMEM),
        compiler_params=PARAMS,
        name="home",
    )(ids_t, *home[0], came_ra, came_la, *home[1], came_rb, came_lb)
    return (
        grad_tokens,
        grad_probs.T.astype(BF16),
        grads[0][None],
        grads[1][None],
        grads[2][None],
    )


def solution(mesh):
    return jax.shard_map(
        on_device,
        mesh=mesh,
        in_specs=(
            P(("dp", "expert"), None),
            P(("dp", "expert"), None),
            P(("dp", "expert"), None),
            P(("dp", "expert"), None),
            P("expert", None, None),
            P("expert", None, None),
            P("expert", None, None),
        ),
        out_specs=(
            P(("dp", "expert"), None),
            P(("dp", "expert"), None),
            P("expert", "dp", None),
            P("expert", "dp", None),
            P("expert", "dp", None),
        ),
        check_vma=False,
    )
```

```python
import functools

import jax
import jax.numpy as jnp
from jax import lax
from jax.experimental import pallas as pl
from jax.experimental.pallas import tpu as pltpu
from jax.sharding import PartitionSpec as P

BF16, F32 = jnp.bfloat16, jnp.float32
ROWS, LANES = 16, 128
VMEM = pl.BlockSpec(memory_space=pltpu.VMEM)
SMEM = pl.BlockSpec(memory_space=pltpu.SMEM)
PARAMS = pltpu.CompilerParams(vmem_limit_bytes=16 * 1024 * 1024)


def iota(shape, dim):
    return lax.broadcasted_iota(jnp.int32, shape, dim)


def nt(a, b):
    return lax.dot_general(a, b, (((1,), (1,)), ((), ())), preferred_element_type=F32)


def put_tiles(ref, first, value):
    rows, width = value.shape
    across = width // LANES
    for i in range(rows // ROWS):
        for j in range(across):
            ref[first + i * across + j] = value[
                i * ROWS : (i + 1) * ROWS, j * LANES : (j + 1) * LANES
            ]


def take_tiles(ref, first, dst, row, rows, width):
    across = width // LANES
    for i in range(rows // ROWS):
        for j in range(across):
            dst[row + i * ROWS : row + (i + 1) * ROWS, j * LANES : (j + 1) * LANES] = ref[
                first + i * across + j
            ]


def pack_kernel(tok_ref, cot_ref, ids_ref, prob_ref, out_ref):
    tok_dev, width = tok_ref.shape
    half = tok_dev // 2
    block = half * width // (ROWS * LANES)
    ids, prob = ids_ref[...], prob_ref[...].astype(F32)
    for i in range(out_ref.shape[1] - 2 * block):
        expert = iota((ROWS, tok_dev), 0) + i * ROWS
        dense = jnp.zeros((ROWS, tok_dev), F32)
        for k in range(ids.shape[0]):
            dense += jnp.where(ids[k : k + 1] == expert, prob[k : k + 1], 0.0)
        for n in range(2):
            out_ref[n, 2 * block + i] = dense.astype(BF16)
    for n in range(2):
        put_tiles(out_ref.at[n], 0, tok_ref[n * half : (n + 1) * half])
        put_tiles(out_ref.at[n], block, cot_ref[n * half : (n + 1) * half])


def expert_kernel(halves, half, *refs):
    me_ref, refs = refs[0], refs[1:]
    packets, refs = refs[: len(halves)], refs[len(halves) :]
    weights, refs = (refs[:3], refs[3:6]), refs[6:]
    grads, refs = refs[: len(halves)], refs[len(halves) :]
    xt_ref, outs, (x_ref, dy_ref) = refs[0], (refs[1:4], refs[4:7]), refs[7:]
    width, ff = weights[0][0].shape
    block = half * width // (ROWS * LANES)
    pieces = [
        (ref.at[i], grad.at[i], which)
        for ref, grad, names in zip(packets, grads, halves)
        for i, which in enumerate(names)
    ]
    extra = packets[0].shape[1] - 2 * block
    eyes = [iota((half, LANES), 0) + n * half == iota((half, LANES), 1) for n in range(2)]
    for n, (ref, _, _) in enumerate(pieces):
        take_tiles(ref, 0, x_ref, n * half, half, width)
        take_tiles(ref, block, dy_ref, n * half, half, width)
    x, dy = x_ref[...], dy_ref[...]
    rows, by_expert = None, [[0.0] * extra for _ in pieces]
    for e, (wg_ref, wu_ref, wd_ref) in enumerate(weights):
        me = me_ref[e]
        mine = [iota((ROWS, LANES), 0) + i * ROWS == me for i in range(extra)]
        probs = []
        for ref, _, which in pieces:
            row = sum(
                jnp.sum(
                    jnp.where(mine[i], ref[2 * block + i].astype(F32), 0.0), axis=0, keepdims=True
                )
                for i in range(extra)
            )
            probs.append(jnp.sum(jnp.where(eyes[which], row, 0.0), axis=1, keepdims=True))
        prob = jnp.concatenate(probs, axis=0)
        gate = jnp.dot(x, wg_ref[...], preferred_element_type=F32)
        up = jnp.dot(x, wu_ref[...], preferred_element_type=F32)
        dz = nt(dy, wd_ref[...])
        sig = jax.nn.sigmoid(gate)
        act, dact = gate * sig, sig + gate * sig * (1.0 - sig)
        hidden = (act * up).astype(BF16)
        gate_grad = jnp.sum(dz * hidden.astype(F32), axis=1, keepdims=True)
        dh = prob * dz
        d_gate = (dh * up * dact).astype(BF16)
        d_up = (dh * act).astype(BF16)
        back = nt(d_gate, wg_ref[...]) + nt(d_up, wu_ref[...])
        rows = back if rows is None else rows + back
        for n, (_, _, which) in enumerate(pieces):
            row = jnp.sum(
                jnp.where(eyes[which], gate_grad[n * half : (n + 1) * half], 0.0),
                axis=0,
                keepdims=True,
            )
            for i in range(extra):
                by_expert[n][i] += jnp.where(mine[i], row, 0.0)
        dgu_ref, ht_ref, sc_ref = outs[e]
        dgu_ref[:, :ff] = d_gate
        dgu_ref[:, ff:] = d_up
        ht_ref[...] = hidden.T
        sc_ref[...] = (prob * dy.astype(F32)).astype(BF16)
    for n, (_, grad, _) in enumerate(pieces):
        put_tiles(grad, 0, rows[n * half : (n + 1) * half].astype(BF16))
        for i in range(extra):
            grad[block + i] = by_expert[n][i].astype(BF16)
    xt_ref[...] = x.T


def weight_kernel(groups, start, extra, final, *refs):
    refs = refs[1:]
    total_w = total_d = None
    for n in range(start + extra):
        w, d = refs[0][...].astype(F32), refs[1][...].astype(F32)
        total_w = w if total_w is None else total_w + w
        total_d = d if total_d is None else total_d + d
        refs = refs[2:]
    for g in range(groups):
        xt, dgu, ht, sc = refs[4 * g : 4 * g + 4]
        w = jnp.dot(xt[...], dgu[...], preferred_element_type=F32)
        d = jnp.dot(ht[...], sc[...], preferred_element_type=F32)
        total_w = w if total_w is None else total_w + w
        total_d = d if total_d is None else total_d + d
    out_w, out_d = refs[4 * groups :]
    out_w[...] = total_w.astype(out_w.dtype)
    out_d[...] = total_d.astype(out_d.dtype)


def weight_sums(totals, groups, width, ff, part=None, parts=1, extra=None, kind=F32):
    steps = 4 // parts
    tile_w, tile_d = width // 4, ff // 4
    first = jnp.zeros((1,), jnp.int32) if part is None else (part * steps).astype(jnp.int32)[None]
    row = lambda i, s: (s[0] + i, 0)
    whole = lambda i, s: (0, 0)
    out_row = lambda i, s: (i, 0)
    blocks = ((tile_w, 2 * ff), (tile_d, width))
    specs, args = [], []
    if totals is not None:
        specs += [pl.BlockSpec(b, row) for b in blocks]
        args += list(totals)
    if extra is not None:
        specs += [pl.BlockSpec(b, out_row) for b in blocks]
        args += list(extra)
    for xt, dgu, ht, sc in groups:
        k = xt.shape[1]
        specs += [
            pl.BlockSpec((tile_w, k), row),
            pl.BlockSpec((k, 2 * ff), whole),
            pl.BlockSpec((tile_d, k), row),
            pl.BlockSpec((k, width), whole),
        ]
        args += [xt, dgu, ht, sc]
    rows = sum(g[0].shape[1] for g in groups)
    return pl.pallas_call(
        functools.partial(
            weight_kernel, len(groups), int(totals is not None), int(extra is not None), kind
        ),
        out_shape=tuple(jax.ShapeDtypeStruct((r * steps, c), kind) for r, c in blocks),
        grid_spec=pltpu.PrefetchScalarGridSpec(
            num_scalar_prefetch=1,
            grid=(steps,),
            in_specs=specs,
            out_specs=tuple(pl.BlockSpec(b, out_row) for b in blocks),
        ),
        compiler_params=PARAMS,
        cost_estimate=pl.CostEstimate(
            flops=6 * rows * width * ff // parts, bytes_accessed=8 * 2**20 // parts, transcendentals=0
        ),
        name="weight_sums",
    )(first, *args)


def home_kernel(count, ids_ref, *refs):
    out_ref, prob_ref = refs[count:]
    tok_dev, width = out_ref.shape
    half = tok_dev // 2
    block = half * width // (ROWS * LANES)
    across = width // LANES
    sums = []
    for n in range(2):
        total = sum(ref[n].astype(F32) for ref in refs[:count])
        for i in range(half // ROWS):
            for j in range(across):
                out_ref[
                    n * half + i * ROWS : n * half + (i + 1) * ROWS, j * LANES : (j + 1) * LANES
                ] = total[i * across + j].astype(BF16)
        sums.append(total[block:])
    by_expert = sums[0] + sums[1]
    ids = ids_ref[...]
    for k in range(ids.shape[0]):
        row = jnp.zeros((1, tok_dev), F32)
        for i in range(by_expert.shape[0]):
            expert = iota((ROWS, tok_dev), 0) + i * ROWS
            row += jnp.sum(
                jnp.where(ids[k : k + 1] == expert, by_expert[i], 0.0), axis=0, keepdims=True
            )
        prob_ref[k : k + 1] = row


def on_device(tokens, cotangent, expert_ids, gate_probs, w_gate, w_up, w_down):
    tok_dev, width = tokens.shape
    ff = w_gate.shape[2]
    half = tok_dev // 2
    devices = lax.axis_size("expert")
    groups = lax.axis_size("dp")
    experts = devices * w_gate.shape[0]
    block = half * width // (ROWS * LANES)
    extra = experts // ROWS

    chips = devices // 2
    ring = list(range(0, chips, 2)) + list(range(1, chips, 2))[::-1]
    hop = {
        d: [
            (2 * ring[i] + c, 2 * ring[(i + d) % chips] + c)
            for i in range(chips)
            for c in range(2)
        ]
        for d in (1, -1)
    }
    right = lambda v: lax.ppermute(v, "expert", hop[1])
    left = lambda v: lax.ppermute(v, "expert", hop[-1])
    swap = lambda v: lax.ppermute(v, "expert", [(i, i ^ 1) for i in range(devices)])
    full, odd = (chips - 1) // 2, chips % 2 == 0

    me = lax.axis_index("expert").astype(jnp.int32)
    pair = jnp.stack([me, me ^ 1])
    ids_t, probs_t = expert_ids.T, gate_probs.T
    own = (w_gate[0], w_up[0], w_down[0])

    whole = lambda v: pl.BlockSpec(v.shape, lambda i: (0,) * len(v.shape))
    packet = jax.ShapeDtypeStruct((2, 2 * block + extra, ROWS, LANES), BF16)
    start = pl.pallas_call(
        pack_kernel,
        grid=(1,),
        out_shape=packet,
        in_specs=[whole(v) for v in (tokens, cotangent, ids_t, probs_t)],
        out_specs=whole(packet),
        compiler_params=PARAMS,
        name="pack",
    )(tokens, cotangent, ids_t, probs_t)

    weights = own + tuple(swap(v) for v in own)

    def expert(*packets, halves):
        rows = half * sum(len(h) for h in halves)
        shape = lambda *s: jax.ShapeDtypeStruct(s, BF16)
        each = (shape(rows, 2 * ff), shape(ff, rows), shape(rows, width))
        outs = pl.pallas_call(
            functools.partial(expert_kernel, halves, half),
            out_shape=tuple(shape(len(h), block + extra, ROWS, LANES) for h in halves)
            + (shape(width, rows),)
            + each * 2,
            in_specs=[SMEM] + [VMEM] * (len(packets) + 6),
            out_specs=(VMEM,) * (len(packets) + 7),
            scratch_shapes=[pltpu.VMEM((rows, width), BF16), pltpu.VMEM((rows, width), BF16)],
            compiler_params=PARAMS,
            cost_estimate=pl.CostEstimate(
                flops=20 * rows * width * ff,
                bytes_accessed=8 * 2**20,
                transcendentals=2 * rows * ff,
            ),
            name="expert",
        )(pair, *packets, *weights)
        grads, xt, rest = outs[: len(packets)], outs[len(packets)], outs[len(packets) + 1 :]
        return grads, ((xt,) + rest[:3], (xt,) + rest[3:])

    both = (0, 1)
    (home,), group = expert(start, halves=(both,))
    group = [group]
    r = l = start
    local = {}
    for s in range(1, full + 1):
        r, l = right(r), left(l)
        local[s], new = expert(r, l, halves=(both, both))
        group.append(new)
    if odd:
        ends = right(r[:1]), left(l[1:])
        local[full + 1], new = expert(*ends, halves=((0,), (1,)))
        group.append(new)

    sums = functools.partial(weight_sums, width=width, ff=ff)
    totals = [None, None]
    for some in (group[:-2], group[-2:-1]):
        for e in range(2):
            totals[e] = sums(totals[e], [g[e] for g in some])
    final = [[g[e] for g in group[-1:]] for e in range(2)]

    def both_cores(**part):
        other = [swap(v) for v in sums(totals[1], final[1], kind=BF16, **part)]
        return sums(totals[0], final[0], kind=BF16, extra=other, **part)

    if groups == 2:
        here = lax.axis_index("dp")
        got = [
            lax.ppermute(v, "dp", [(0, 1), (1, 0)]) for v in both_cores(part=1 - here, parts=2)
        ]
        keep = both_cores(part=here, parts=2)
        grad_w, grad_d = [
            (a.astype(F32) + b.astype(F32)).astype(BF16) for a, b in zip(keep, got)
        ]
    else:
        grad_w, grad_d = [
            lax.psum_scatter(v, "dp", scatter_dimension=0, tiled=True) for v in both_cores()
        ]

    def add(a, b):
        return (a.astype(F32) + b.astype(F32)).astype(BF16)

    def back(side, move):
        moving = None
        if odd:
            moving = move(local[full + 1][side])
        for s in range(full, 0, -1):
            here = local[s][side]
            if moving is None:
                moving = here
            elif moving.shape == here.shape:
                moving = add(moving, here)
            elif side == 0:
                moving = jnp.concatenate([add(moving, here[:1]), here[1:]])
            else:
                moving = jnp.concatenate([here[:1], add(moving, here[1:])])
            moving = move(moving)
        return moving

    parts = (home, back(0, left), back(1, right))
    grad_tokens, grad_probs = pl.pallas_call(
        functools.partial(home_kernel, len(parts)),
        out_shape=(
            jax.ShapeDtypeStruct((tok_dev, width), BF16),
            jax.ShapeDtypeStruct(ids_t.shape, F32),
        ),
        in_specs=[VMEM] * (1 + len(parts)),
        out_specs=(VMEM, VMEM),
        compiler_params=PARAMS,
        name="home",
    )(ids_t, *parts)
    return (
        grad_tokens,
        grad_probs.T.astype(BF16),
        grad_w[None, :, :ff],
        grad_w[None, :, ff:],
        grad_d[None],
    )


def solution(mesh):
    return jax.shard_map(
        on_device,
        mesh=mesh,
        in_specs=(
            P(("dp", "expert"), None),
            P(("dp", "expert"), None),
            P(("dp", "expert"), None),
            P(("dp", "expert"), None),
            P("expert", None, None),
            P("expert", None, None),
            P("expert", None, None),
        ),
        out_specs=(
            P(("dp", "expert"), None),
            P(("dp", "expert"), None),
            P("expert", "dp", None),
            P("expert", "dp", None),
            P("expert", "dp", None),
        ),
        check_vma=False,
    )
```

```python
import functools

import jax
import jax.numpy as jnp
from jax import lax
from jax.experimental import pallas as pl
from jax.experimental.pallas import tpu as pltpu
from jax.sharding import PartitionSpec as P

BF16, F32 = jnp.bfloat16, jnp.float32
ROWS, LANES = 16, 128
VMEM = pl.BlockSpec(memory_space=pltpu.VMEM)
ANY = pl.BlockSpec(memory_space=pl.ANY)
SMEM = pl.BlockSpec(memory_space=pltpu.SMEM)
STEPS = 4
EXPERT_VMEM = 16 * 1024 * 1024
TOKEN = jax.ShapeDtypeStruct((8, LANES), F32)
PARAMS = pltpu.CompilerParams(vmem_limit_bytes=16 * 1024 * 1024)


def iota(shape, dim):
    return lax.broadcasted_iota(jnp.int32, shape, dim)


def kept(*shape, kind=BF16):
    return jax.ShapeDtypeStruct(shape, kind)


def put_tiles(ref, first, value):
    rows, width = value.shape
    across = width // LANES
    for i in range(rows // ROWS):
        for j in range(across):
            ref[first + i * across + j] = value[
                i * ROWS : (i + 1) * ROWS, j * LANES : (j + 1) * LANES
            ]


def take_tiles(ref, first, dst, row, rows, width):
    across = width // LANES
    for i in range(rows // ROWS):
        for j in range(across):
            dst[row + i * ROWS : row + (i + 1) * ROWS, j * LANES : (j + 1) * LANES] = ref[
                first + i * across + j
            ]


def pack_kernel(tok_ref, cot_ref, ids_ref, prob_ref, out_ref, token):
    tok_dev, width = tok_ref.shape
    half = tok_dev // 2
    block = half * width // (ROWS * LANES)
    token[...] = jnp.zeros_like(token)
    ids, prob = ids_ref[...], prob_ref[...].astype(F32)
    for i in range(out_ref.shape[1] - 2 * block):
        expert = iota((ROWS, tok_dev), 0) + i * ROWS
        dense = jnp.zeros((ROWS, tok_dev), F32)
        for k in range(ids.shape[0]):
            dense += jnp.where(ids[k : k + 1] == expert, prob[k : k + 1], 0.0)
        for n in range(2):
            out_ref[n, 2 * block + i] = dense.astype(BF16)
    for n in range(2):
        put_tiles(out_ref.at[n], 0, tok_ref[n * half : (n + 1) * half])
        put_tiles(out_ref.at[n], block, cot_ref[n * half : (n + 1) * half])


def put_strips(ref, e, at, value):
    rows, width = value.shape
    for j in range(width // LANES):
        ref[e, at + j * rows : at + (j + 1) * rows] = value[:, j * LANES : (j + 1) * LANES]


def take_strips(ref, e, at, rows, width):
    return jnp.concatenate(
        [ref[e, at + j * rows : at + (j + 1) * rows] for j in range(width // LANES)], axis=1
    )


def weights_kernel(*refs):
    out_ref = refs[6]
    for e in range(2):
        wg, wu, wd = (ref[...] for ref in refs[3 * e : 3 * e + 3])
        width, ff = wg.shape
        put_strips(out_ref, e, 0, jnp.concatenate([wg, wu], axis=1))
        put_strips(out_ref, e, 2 * ff // LANES * width, wd.T)
        put_strips(out_ref, e, 3 * ff // LANES * width, jnp.concatenate([wg.T, wu.T], axis=0))


def expert_kernel(halves, half, width, ff, start, last, *refs):
    count = len(halves)
    me_ref, refs = refs[0], refs[2:]
    packets, refs = refs[:count], refs[count:]
    weights, refs = refs[0], refs[1:]
    if start:
        before, refs = refs[0], refs[1:]
    grads, refs = refs[:count], refs[count:]
    if not last:
        totals, refs = refs[0], refs[1:]
    token, refs = refs[0], refs[1:]
    xt_ref, outs, (x_ref, dy_ref) = refs[0], (refs[1:4], refs[4:7]), refs[7:]
    token[...] = jnp.zeros_like(token)
    block = half * width // (ROWS * LANES)
    pieces = [
        (ref.at[i], grad.at[i], which)
        for ref, grad, names in zip(packets, grads, halves)
        for i, which in enumerate(names)
    ]
    extra = packets[0].shape[1] - 2 * block
    eyes = [iota((half, LANES), 0) + n * half == iota((half, LANES), 1) for n in range(2)]
    for n, (ref, _, _) in enumerate(pieces):
        take_tiles(ref, 0, x_ref, n * half, half, width)
        take_tiles(ref, block, dy_ref, n * half, half, width)
    x, dy = x_ref[...], dy_ref[...]
    rows, by_expert = None, [[0.0] * extra for _ in pieces]
    for e in range(2):
        w_gu = take_strips(weights, e, 0, width, 2 * ff)
        w_d_t = take_strips(weights, e, 2 * ff // LANES * width, width, ff)
        w_gu_t = take_strips(weights, e, 3 * ff // LANES * width, 2 * ff, width)
        me = me_ref[e]
        mine = [iota((ROWS, LANES), 0) + i * ROWS == me for i in range(extra)]
        probs = []
        for ref, _, which in pieces:
            row = sum(
                jnp.sum(
                    jnp.where(mine[i], ref[2 * block + i].astype(F32), 0.0), axis=0, keepdims=True
                )
                for i in range(extra)
            )
            probs.append(jnp.sum(jnp.where(eyes[which], row, 0.0), axis=1, keepdims=True))
        prob = jnp.concatenate(probs, axis=0)
        both = jnp.dot(x, w_gu, preferred_element_type=F32)
        gate, up = both[:, :ff], both[:, ff:]
        dz = jnp.dot(dy, w_d_t, preferred_element_type=F32)
        sig = jax.nn.sigmoid(gate)
        act, dact = gate * sig, sig + gate * sig * (1.0 - sig)
        hidden = (act * up).astype(BF16)
        gate_grad = jnp.sum(dz * hidden.astype(F32), axis=1, keepdims=True)
        dh = prob * dz
        d_gate = (dh * up * dact).astype(BF16)
        d_up = (dh * act).astype(BF16)
        d_both = jnp.concatenate([d_gate, d_up], axis=1)
        back = jnp.dot(d_both, w_gu_t, preferred_element_type=F32)
        rows = back if rows is None else rows + back
        for n, (_, _, which) in enumerate(pieces):
            row = jnp.sum(
                jnp.where(eyes[which], gate_grad[n * half : (n + 1) * half], 0.0),
                axis=0,
                keepdims=True,
            )
            for i in range(extra):
                by_expert[n][i] += jnp.where(mine[i], row, 0.0)
        dgu_ref, ht_ref, sc_ref = outs[e]
        dgu_ref[...] = d_both
        ht_ref[...] = hidden.T
        sc_ref[...] = (prob * dy.astype(F32)).astype(BF16)
    for n, (_, grad, _) in enumerate(pieces):
        put_tiles(grad, 0, rows[n * half : (n + 1) * half].astype(BF16))
        for i in range(extra):
            grad[block + i] = by_expert[n][i].astype(BF16)
    xt_ref[...] = x.T
    if not last:
        for e, (dgu_ref, ht_ref, sc_ref) in enumerate(outs):
            at = 0
            for a, b in ((xt_ref, dgu_ref), (ht_ref, sc_ref)):
                rows = a.shape[0]
                tile = rows // STEPS
                for step in range(STEPS):
                    new = jnp.dot(
                        a[step * tile : (step + 1) * tile], b[...], preferred_element_type=F32
                    )
                    for j in range(b.shape[1] // LANES):
                        to = pl.ds(at + j * rows + step * tile, tile)
                        strip = new[:, j * LANES : (j + 1) * LANES]
                        totals[e, to] = before[e, to] + strip if start else strip
                at += rows * b.shape[1] // LANES


def weight_kernel(steps, part_ref, turn_ref, *refs):
    totals, xt, refs = refs[0], refs[1], refs[2:]
    groups, outs, token = (refs[:3], refs[3:6]), refs[6:8], refs[8]
    token[...] = jnp.zeros_like(token)
    for e, (dgu, ht, sc) in enumerate(groups):
        to = 0
        for step in range(steps):
            at = 0
            for a, b in ((xt, dgu), (ht, sc)):
                rows, across = a.shape[0], b.shape[1] // LANES
                tile = rows // STEPS
                first = pl.multiple_of((part_ref[0] * steps + step) * tile, tile)
                new = jnp.dot(a[pl.ds(first, tile)], b[...], preferred_element_type=F32)
                for j in range(across):
                    strip = new[:, j * LANES : (j + 1) * LANES]
                    strip += totals[e, pl.ds(at + j * rows + first, tile)]
                    for i in range(tile // ROWS):
                        outs[e][to + i * across + j] = strip[i * ROWS : (i + 1) * ROWS].astype(
                            BF16
                        )
                at += rows * across
                to += tile // ROWS * across


def weight_sums(turn, totals, group, part, parts):
    tiles = totals.size // (2 * parts * ROWS * LANES)
    return pl.pallas_call(
        functools.partial(weight_kernel, STEPS // parts),
        out_shape=(kept(tiles, ROWS, LANES),) * 2 + (TOKEN,),
        in_specs=[SMEM, ANY] + [VMEM] * (1 + len(group)),
        out_specs=(VMEM,) * 3,
        compiler_params=PARAMS,
        cost_estimate=pl.CostEstimate(
            flops=2 * totals.size * group[0].shape[1] // parts,
            bytes_accessed=16 * 2**20 // parts,
            transcendentals=0,
        ),
        name="weight_sums",
    )(part.astype(jnp.int32)[None], turn, totals, *group)


def finish_kernel(count, *refs):
    outs = refs[count:]
    width, ff = outs[2].shape[1], outs[0].shape[1]
    tile_w, tile_d = width // STEPS, ff // STEPS
    across_w, across_d = 2 * ff // LANES, width // LANES
    each = ff // LANES
    n = 0
    for step in range(outs[0].shape[0] // tile_w):
        for i in range(tile_w // ROWS):
            rows = slice(step * tile_w + i * ROWS, step * tile_w + (i + 1) * ROWS)
            for j in range(across_w):
                total = sum(ref[n + j].astype(F32) for ref in refs[:count]).astype(BF16)
                at = slice(j % each * LANES, (j % each + 1) * LANES)
                outs[j // each][rows, at] = total
            n += across_w
        for i in range(tile_d // ROWS):
            rows = slice(step * tile_d + i * ROWS, step * tile_d + (i + 1) * ROWS)
            for j in range(across_d):
                total = sum(ref[n + j].astype(F32) for ref in refs[:count]).astype(BF16)
                outs[2][rows, j * LANES : (j + 1) * LANES] = total
            n += across_d


def home_kernel(count, ids_ref, *refs):
    out_ref, prob_ref = refs[count:]
    tok_dev, width = out_ref.shape
    half = tok_dev // 2
    block = half * width // (ROWS * LANES)
    across = width // LANES
    sums = []
    for n in range(2):
        total = sum(ref[n].astype(F32) for ref in refs[:count])
        for i in range(half // ROWS):
            for j in range(across):
                out_ref[
                    n * half + i * ROWS : n * half + (i + 1) * ROWS, j * LANES : (j + 1) * LANES
                ] = total[i * across + j].astype(BF16)
        sums.append(total[block:])
    by_expert = sums[0] + sums[1]
    ids = ids_ref[...]
    for k in range(ids.shape[0]):
        row = jnp.zeros((1, tok_dev), F32)
        for i in range(by_expert.shape[0]):
            expert = iota((ROWS, tok_dev), 0) + i * ROWS
            row += jnp.sum(
                jnp.where(ids[k : k + 1] == expert, by_expert[i], 0.0), axis=0, keepdims=True
            )
        prob_ref[k : k + 1] = row


def on_device(tokens, cotangent, expert_ids, gate_probs, w_gate, w_up, w_down):
    tok_dev, width = tokens.shape
    ff = w_gate.shape[2]
    half = tok_dev // 2
    devices = lax.axis_size("expert")
    groups = lax.axis_size("dp")
    experts = devices * w_gate.shape[0]
    block = half * width // (ROWS * LANES)
    extra = experts // ROWS

    chips = devices // 2
    ring = list(range(0, chips, 2)) + list(range(1, chips, 2))[::-1]
    hop = {
        d: [
            (2 * ring[i] + c, 2 * ring[(i + d) % chips] + c)
            for i in range(chips)
            for c in range(2)
        ]
        for d in (1, -1)
    }
    right = lambda v: lax.ppermute(v, "expert", hop[1])
    left = lambda v: lax.ppermute(v, "expert", hop[-1])
    swap = lambda v: lax.ppermute(v, "expert", [(i, i ^ 1) for i in range(devices)])
    full, odd = (chips - 1) // 2, chips % 2 == 0

    me = lax.axis_index("expert").astype(jnp.int32)
    pair = jnp.stack([me, me ^ 1])
    ids_t, probs_t = expert_ids.T, gate_probs.T
    own = (w_gate[0], w_up[0], w_down[0])

    whole = lambda v: pl.BlockSpec(v.shape, lambda i: (0,) * len(v.shape))
    packet = jax.ShapeDtypeStruct((2, 2 * block + extra, ROWS, LANES), BF16)
    start, turn = pl.pallas_call(
        pack_kernel,
        grid=(1,),
        out_shape=(packet, TOKEN),
        in_specs=[whole(v) for v in (tokens, cotangent, ids_t, probs_t)],
        out_specs=(whole(packet), whole(TOKEN)),
        compiler_params=PARAMS,
        name="pack",
    )(*(pltpu.with_memory_space_constraint(v, pltpu.HBM) for v in (tokens, cotangent, ids_t, probs_t)))

    raw = own + tuple(swap(v) for v in own)
    weights = pl.pallas_call(
        weights_kernel,
        out_shape=kept(2, 5 * ff // LANES * width, LANES),
        in_specs=[VMEM] * 6,
        out_specs=VMEM,
        compiler_params=PARAMS,
        cost_estimate=pl.CostEstimate(flops=0, bytes_accessed=24 * width * ff, transcendentals=0),
        name="weights",
    )(*raw)

    def expert(turn, *packets, halves, totals=None, last=False):
        rows = half * sum(len(h) for h in halves)
        count = len(packets)
        groups = [(width, rows)] + [(rows, 2 * ff), (ff, rows), (rows, width)] * 2
        sums = (kept(2, 3 * ff // LANES * width, LANES, kind=F32),)
        start = totals is not None and not last
        out_shape = tuple(kept(len(h), block + extra, ROWS, LANES) for h in halves)
        out_shape += () if last else sums
        out_shape += (TOKEN,)
        scratch = [(rows, width), (rows, width)]
        if last:
            out_shape += tuple(kept(*s) for s in groups)
        else:
            scratch = groups + scratch
        inputs = (pair, turn, *packets, weights) + ((totals,) if start else ())
        outs = pl.pallas_call(
            functools.partial(expert_kernel, halves, half, width, ff, start, last),
            out_shape=out_shape,
            in_specs=[SMEM, ANY] + [VMEM] * (len(inputs) - 2),
            out_specs=(VMEM,) * len(out_shape),
            scratch_shapes=[pltpu.VMEM(s, BF16) for s in scratch],

            compiler_params=pltpu.CompilerParams(vmem_limit_bytes=EXPERT_VMEM),
            cost_estimate=pl.CostEstimate(
                flops=(20 if last else 32) * rows * width * ff,
                bytes_accessed=8 * 2**20,
                transcendentals=2 * rows * ff,
            ),
            name="expert",
        )(*inputs)
        grads, outs = outs[:count], outs[count:]
        if last:
            return grads, outs[1:], outs[0]
        return grads, outs[0], outs[1]

    both = (0, 1)
    totals = None
    r, l = right(start), left(start)
    (home,), totals, turn = expert(turn, start, halves=(both,))
    local = {}
    for s in range(1, full + 1):
        came = r, l
        r, l, turn = lax.optimization_barrier((r, l, turn))
        if s < full:
            r, l = right(r), left(l)
        elif odd:
            ends = right(r[:1]), left(l[1:])
        local[s], totals, turn = expert(turn, *came, halves=(both, both), totals=totals)
    assert odd, "even ring"
    *ends, turn = lax.optimization_barrier((*ends, turn))
    local[full + 1], group, turn = expert(turn, *ends, halves=((0,), (1,)), last=True)

    def add(*terms):
        return sum(t.astype(F32) for t in terms).astype(BF16)

    if groups == 2:
        here = lax.axis_index("dp")
        mine, other, turn = weight_sums(turn, totals, group, 1 - here, 2)
        send = add(mine, swap(other))
        mine, other, turn = weight_sums(turn, totals, group, here, 2)
        got = lax.ppermute(send, "dp", [(0, 1), (1, 0)])
        terms = (mine, swap(other), got)
        shape = lambda *s: jax.ShapeDtypeStruct(s, BF16)
        grads = pl.pallas_call(
            functools.partial(finish_kernel, len(terms)),
            out_shape=(shape(width // 2, ff), shape(width // 2, ff), shape(ff // 2, width)),
            in_specs=[VMEM] * len(terms),
            out_specs=(VMEM,) * 3,
            compiler_params=PARAMS,
            name="finish",
        )(*terms)
    else:
        mine, other, turn = weight_sums(turn, totals, group, jnp.int32(0), 1)
        terms = (add(mine, swap(other)),)
        shape = lambda *s: jax.ShapeDtypeStruct(s, BF16)
        grads = pl.pallas_call(
            functools.partial(finish_kernel, len(terms)),
            out_shape=(shape(width, ff), shape(width, ff), shape(ff, width)),
            in_specs=[VMEM] * len(terms),
            out_specs=(VMEM,) * 3,
            compiler_params=PARAMS,
            name="finish",
        )(*terms)
        grads = [lax.psum_scatter(v, "dp", scatter_dimension=0, tiled=True) for v in grads]

    def back(side, move):
        moving = None
        if odd:
            moving = move(local[full + 1][side])
        for s in range(full, 0, -1):
            here = local[s][side]
            if moving is None:
                moving = here
            else:
                if moving.shape != here.shape:
                    at = [(0, 1), (1, 0)][side]
                    moving = jnp.pad(moving, [at] + [(0, 0)] * (moving.ndim - 1))
                moving = add(moving, here)
            moving = move(moving)
        return moving

    parts = (home, back(0, left), back(1, right))
    grad_tokens, grad_probs = pl.pallas_call(
        functools.partial(home_kernel, len(parts)),
        out_shape=(
            jax.ShapeDtypeStruct((tok_dev, width), BF16),
            jax.ShapeDtypeStruct(ids_t.shape, F32),
        ),
        in_specs=[VMEM] * (1 + len(parts)),
        out_specs=(VMEM, VMEM),
        compiler_params=PARAMS,
        name="home",
    )(ids_t, *parts)
    return (
        grad_tokens,
        grad_probs.T.astype(BF16),
        *(v[None] for v in grads),
    )


def solution(mesh):
    return jax.shard_map(
        on_device,
        mesh=mesh,
        in_specs=(
            P(("dp", "expert"), None),
            P(("dp", "expert"), None),
            P(("dp", "expert"), None),
            P(("dp", "expert"), None),
            P("expert", None, None),
            P("expert", None, None),
            P("expert", None, None),
        ),
        out_specs=(
            P(("dp", "expert"), None),
            P(("dp", "expert"), None),
            P("expert", "dp", None),
            P("expert", "dp", None),
            P("expert", "dp", None),
        ),
        check_vma=False,
    )
```

```python
import functools

import jax
import jax.numpy as jnp
from jax import lax
from jax.experimental import pallas as pl
from jax.experimental.pallas import tpu as pltpu
from jax.sharding import PartitionSpec as P

BF16, F32 = jnp.bfloat16, jnp.float32
ROWS, LANES = 16, 128
VMEM = pl.BlockSpec(memory_space=pltpu.VMEM)
ANY = pl.BlockSpec(memory_space=pl.ANY)
STEPS = 4
EXPERT_VMEM = 16 * 1024 * 1024
TOKEN = jax.ShapeDtypeStruct((8, LANES), F32)
PARAMS = pltpu.CompilerParams(vmem_limit_bytes=16 * 1024 * 1024)


def iota(shape, dim):
    return lax.broadcasted_iota(jnp.int32, shape, dim)


def kept(*shape, kind=BF16):
    return jax.ShapeDtypeStruct(shape, kind)


def put_tiles(ref, first, value):
    rows, width = value.shape
    across = width // LANES
    for i in range(rows // ROWS):
        for j in range(across):
            ref[first + i * across + j] = value[
                i * ROWS : (i + 1) * ROWS, j * LANES : (j + 1) * LANES
            ]


def take_tiles(ref, first, dst, row, rows, width):
    across = width // LANES
    for i in range(rows // ROWS):
        for j in range(across):
            dst[row + i * ROWS : row + (i + 1) * ROWS, j * LANES : (j + 1) * LANES] = ref[
                first + i * across + j
            ]


def pack_kernel(tok_ref, cot_ref, ids_ref, prob_ref, out_ref, token):
    tok_dev, width = tok_ref.shape
    half = tok_dev // 2
    block = half * width // (ROWS * LANES)
    token[...] = jnp.zeros_like(token)
    ids, prob = ids_ref[...], prob_ref[...].astype(F32)
    for i in range(out_ref.shape[1] - 2 * block):
        expert = iota((ROWS, tok_dev), 0) + i * ROWS
        dense = jnp.zeros((ROWS, tok_dev), F32)
        for k in range(ids.shape[0]):
            dense += jnp.where(ids[k : k + 1] == expert, prob[k : k + 1], 0.0)
        for n in range(2):
            out_ref[n, 2 * block + i] = dense.astype(BF16)
    for n in range(2):
        put_tiles(out_ref.at[n], 0, tok_ref[n * half : (n + 1) * half])
        put_tiles(out_ref.at[n], block, cot_ref[n * half : (n + 1) * half])


def put_strips(ref, e, at, value):
    rows, width = value.shape
    for j in range(width // LANES):
        ref[e, at + j * rows : at + (j + 1) * rows] = value[:, j * LANES : (j + 1) * LANES]


def take_strips(ref, e, at, rows, width):
    return jnp.concatenate(
        [ref[e, at + j * rows : at + (j + 1) * rows] for j in range(width // LANES)], axis=1
    )


def weights_kernel(*refs):
    out_ref = refs[6]
    for e in range(2):
        wg, wu, wd = (ref[...] for ref in refs[3 * e : 3 * e + 3])
        width, ff = wg.shape
        put_strips(out_ref, e, 0, jnp.concatenate([wg, wu], axis=1))
        put_strips(out_ref, e, 2 * ff // LANES * width, wd.T)
        put_strips(out_ref, e, 3 * ff // LANES * width, jnp.concatenate([wg.T, wu.T], axis=0))


def expert_kernel(halves, half, width, ff, start, last, *refs):
    count = len(halves)
    me = lax.axis_index("expert")
    refs = refs[1:]
    packets, refs = refs[:count], refs[count:]
    weights, refs = refs[0], refs[1:]
    if start:
        before, refs = refs[0], refs[1:]
    grads, refs = refs[:count], refs[count:]
    if not last:
        totals, refs = refs[0], refs[1:]
    token, refs = refs[0], refs[1:]
    xt_ref, outs, (x_ref, dy_ref) = refs[0], (refs[1:4], refs[4:7]), refs[7:]
    token[...] = jnp.zeros_like(token)
    block = half * width // (ROWS * LANES)
    pieces = [
        (ref.at[i], grad.at[i], which)
        for ref, grad, names in zip(packets, grads, halves)
        for i, which in enumerate(names)
    ]
    extra = packets[0].shape[1] - 2 * block
    eyes = [iota((half, LANES), 0) + n * half == iota((half, LANES), 1) for n in range(2)]
    for n, (ref, _, _) in enumerate(pieces):
        take_tiles(ref, 0, x_ref, n * half, half, width)
        take_tiles(ref, block, dy_ref, n * half, half, width)
    x, dy = x_ref[...], dy_ref[...]
    rows, by_expert = None, [[0.0] * extra for _ in pieces]
    for e in range(2):
        w_gu = take_strips(weights, e, 0, width, 2 * ff)
        w_d_t = take_strips(weights, e, 2 * ff // LANES * width, width, ff)
        w_gu_t = take_strips(weights, e, 3 * ff // LANES * width, 2 * ff, width)
        mine = [iota((ROWS, LANES), 0) + i * ROWS == me ^ e for i in range(extra)]
        probs = []
        for ref, _, which in pieces:
            row = sum(
                jnp.sum(
                    jnp.where(mine[i], ref[2 * block + i].astype(F32), 0.0), axis=0, keepdims=True
                )
                for i in range(extra)
            )
            probs.append(jnp.sum(jnp.where(eyes[which], row, 0.0), axis=1, keepdims=True))
        prob = jnp.concatenate(probs, axis=0)
        both = jnp.dot(x, w_gu, preferred_element_type=F32)
        gate, up = both[:, :ff], both[:, ff:]
        dz = jnp.dot(dy, w_d_t, preferred_element_type=F32)
        sig = jax.nn.sigmoid(gate)
        act, dact = gate * sig, sig + gate * sig * (1.0 - sig)
        hidden = (act * up).astype(BF16)
        gate_grad = jnp.sum(dz * hidden.astype(F32), axis=1, keepdims=True)
        dh = prob * dz
        d_gate = (dh * up * dact).astype(BF16)
        d_up = (dh * act).astype(BF16)
        d_both = jnp.concatenate([d_gate, d_up], axis=1)
        back = jnp.dot(d_both, w_gu_t, preferred_element_type=F32)
        rows = back if rows is None else rows + back
        for n, (_, _, which) in enumerate(pieces):
            row = jnp.sum(
                jnp.where(eyes[which], gate_grad[n * half : (n + 1) * half], 0.0),
                axis=0,
                keepdims=True,
            )
            for i in range(extra):
                by_expert[n][i] += jnp.where(mine[i], row, 0.0)
        dgu_ref, ht_ref, sc_ref = outs[e]
        dgu_ref[...] = d_both
        ht_ref[...] = hidden.T
        sc_ref[...] = (prob * dy.astype(F32)).astype(BF16)
    for n, (_, grad, _) in enumerate(pieces):
        put_tiles(grad, 0, rows[n * half : (n + 1) * half].astype(BF16))
        for i in range(extra):
            grad[block + i] = by_expert[n][i].astype(BF16)
    xt_ref[...] = x.T
    if not last:
        for e, (dgu_ref, ht_ref, sc_ref) in enumerate(outs):
            at = 0
            for a, b in ((xt_ref, dgu_ref), (ht_ref, sc_ref)):
                rows = a.shape[0]
                tile = rows // STEPS
                for step in range(STEPS):
                    new = jnp.dot(
                        a[step * tile : (step + 1) * tile], b[...], preferred_element_type=F32
                    )
                    for j in range(b.shape[1] // LANES):
                        to = pl.ds(at + j * rows + step * tile, tile)
                        strip = new[:, j * LANES : (j + 1) * LANES]
                        totals[e, to] = before[e, to] + strip if start else strip
                at += rows * b.shape[1] // LANES


def weight_kernel(steps, away, turn_ref, *refs):
    totals, xt, refs = refs[0], refs[1], refs[2:]
    groups, outs, token = (refs[:3], refs[3:6]), refs[6:8], refs[8]
    part = 0 if away is None else lax.axis_index("dp") ^ away
    token[...] = jnp.zeros_like(token)
    for e, (dgu, ht, sc) in enumerate(groups):
        to = 0
        for step in range(steps):
            at = 0
            for a, b in ((xt, dgu), (ht, sc)):
                rows, across = a.shape[0], b.shape[1] // LANES
                tile = rows // STEPS
                first = pl.multiple_of((part * steps + step) * tile, tile)
                new = jnp.dot(a[pl.ds(first, tile)], b[...], preferred_element_type=F32)
                for j in range(across):
                    strip = new[:, j * LANES : (j + 1) * LANES]
                    strip += totals[e, pl.ds(at + j * rows + first, tile)]
                    for i in range(tile // ROWS):
                        outs[e][to + i * across + j] = strip[i * ROWS : (i + 1) * ROWS].astype(
                            BF16
                        )
                at += rows * across
                to += tile // ROWS * across


def weight_sums(turn, totals, group, away=None):
    parts = 1 if away is None else 2
    tiles = totals.size // (2 * parts * ROWS * LANES)
    return pl.pallas_call(
        functools.partial(weight_kernel, STEPS // parts, away),
        out_shape=(kept(tiles, ROWS, LANES),) * 2 + (TOKEN,),
        in_specs=[ANY] + [VMEM] * (1 + len(group)),
        out_specs=(VMEM,) * 3,
        compiler_params=PARAMS,
        cost_estimate=pl.CostEstimate(
            flops=2 * totals.size * group[0].shape[1] // parts,
            bytes_accessed=16 * 2**20 // parts,
            transcendentals=0,
        ),
        name="weight_sums",
    )(turn, totals, *group)


def finish_kernel(count, *refs):
    outs, token = refs[count:-1], refs[-1]
    token[...] = jnp.zeros_like(token)
    width, ff = outs[2].shape[1], outs[0].shape[1]
    tile_w, tile_d = width // STEPS, ff // STEPS
    across_w, across_d = 2 * ff // LANES, width // LANES
    each = ff // LANES
    n = 0
    for step in range(outs[0].shape[0] // tile_w):
        for i in range(tile_w // ROWS):
            rows = slice(step * tile_w + i * ROWS, step * tile_w + (i + 1) * ROWS)
            for j in range(across_w):
                total = sum(ref[n + j].astype(F32) for ref in refs[:count]).astype(BF16)
                at = slice(j % each * LANES, (j % each + 1) * LANES)
                outs[j // each][rows, at] = total
            n += across_w
        for i in range(tile_d // ROWS):
            rows = slice(step * tile_d + i * ROWS, step * tile_d + (i + 1) * ROWS)
            for j in range(across_d):
                total = sum(ref[n + j].astype(F32) for ref in refs[:count]).astype(BF16)
                outs[2][rows, j * LANES : (j + 1) * LANES] = total
            n += across_d


def home_kernel(count, turn_ref, ids_ref, *refs):
    out_ref, prob_ref = refs[count:]
    tok_dev, width = out_ref.shape
    half = tok_dev // 2
    block = half * width // (ROWS * LANES)
    across = width // LANES
    sums = []
    for n in range(2):
        total = sum(ref[n].astype(F32) for ref in refs[:count])
        for i in range(half // ROWS):
            for j in range(across):
                out_ref[
                    n * half + i * ROWS : n * half + (i + 1) * ROWS, j * LANES : (j + 1) * LANES
                ] = total[i * across + j].astype(BF16)
        sums.append(total[block:])
    by_expert = sums[0] + sums[1]
    ids = ids_ref[...]
    for k in range(ids.shape[0]):
        row = jnp.zeros((1, tok_dev), F32)
        for i in range(by_expert.shape[0]):
            expert = iota((ROWS, tok_dev), 0) + i * ROWS
            row += jnp.sum(
                jnp.where(ids[k : k + 1] == expert, by_expert[i], 0.0), axis=0, keepdims=True
            )
        prob_ref[k : k + 1] = row


def on_device(tokens, cotangent, expert_ids, gate_probs, w_gate, w_up, w_down):
    tok_dev, width = tokens.shape
    ff = w_gate.shape[2]
    half = tok_dev // 2
    devices = lax.axis_size("expert")
    groups = lax.axis_size("dp")
    experts = devices * w_gate.shape[0]
    block = half * width // (ROWS * LANES)
    extra = experts // ROWS

    chips = devices // 2
    ring = list(range(0, chips, 2)) + list(range(1, chips, 2))[::-1]
    hop = {
        d: [
            (2 * ring[i] + c, 2 * ring[(i + d) % chips] + c)
            for i in range(chips)
            for c in range(2)
        ]
        for d in (1, -1)
    }
    right = lambda v: lax.ppermute(v, "expert", hop[1])
    left = lambda v: lax.ppermute(v, "expert", hop[-1])
    swap = lambda v: lax.ppermute(v, "expert", [(i, i ^ 1) for i in range(devices)])
    full, odd = (chips - 1) // 2, chips % 2 == 0

    ids_t, probs_t = expert_ids.T, gate_probs.T
    own = (w_gate[0], w_up[0], w_down[0])

    whole = lambda v: pl.BlockSpec(v.shape, lambda i: (0,) * len(v.shape))
    packet = jax.ShapeDtypeStruct((2, 2 * block + extra, ROWS, LANES), BF16)
    start, turn = pl.pallas_call(
        pack_kernel,
        grid=(1,),
        out_shape=(packet, TOKEN),
        in_specs=[whole(v) for v in (tokens, cotangent, ids_t, probs_t)],
        out_specs=(whole(packet), whole(TOKEN)),
        compiler_params=PARAMS,
        name="pack",
    )(*(pltpu.with_memory_space_constraint(v, pltpu.HBM) for v in (tokens, cotangent, ids_t, probs_t)))

    raw = own + tuple(swap(v) for v in own)
    weights = pl.pallas_call(
        weights_kernel,
        out_shape=kept(2, 5 * ff // LANES * width, LANES),
        in_specs=[VMEM] * 6,
        out_specs=VMEM,
        compiler_params=PARAMS,
        cost_estimate=pl.CostEstimate(flops=0, bytes_accessed=24 * width * ff, transcendentals=0),
        name="weights",
    )(*raw)

    def expert(turn, *packets, halves, totals=None, last=False):
        rows = half * sum(len(h) for h in halves)
        count = len(packets)
        groups = [(width, rows)] + [(rows, 2 * ff), (ff, rows), (rows, width)] * 2
        sums = (kept(2, 3 * ff // LANES * width, LANES, kind=F32),)
        start = totals is not None and not last
        out_shape = tuple(kept(len(h), block + extra, ROWS, LANES) for h in halves)
        out_shape += () if last else sums
        out_shape += (TOKEN,)
        scratch = [(rows, width), (rows, width)]
        if last:
            out_shape += tuple(kept(*s) for s in groups)
        else:
            scratch = groups + scratch
        inputs = (turn, *packets, weights) + ((totals,) if start else ())
        outs = pl.pallas_call(
            functools.partial(expert_kernel, halves, half, width, ff, start, last),
            out_shape=out_shape,
            in_specs=[ANY] + [VMEM] * (len(inputs) - 1),
            out_specs=(VMEM,) * len(out_shape),
            scratch_shapes=[pltpu.VMEM(s, BF16) for s in scratch],

            compiler_params=pltpu.CompilerParams(vmem_limit_bytes=EXPERT_VMEM),
            cost_estimate=pl.CostEstimate(
                flops=(20 if last else 32) * rows * width * ff,
                bytes_accessed=8 * 2**20,
                transcendentals=2 * rows * ff,
            ),
            name="expert",
        )(*inputs)
        grads, outs = outs[:count], outs[count:]
        if last:
            return grads, outs[1:], outs[0]
        return grads, outs[0], outs[1]

    both = (0, 1)
    totals = None
    r, l = right(start), left(start)
    (home,), totals, turn = expert(turn, start, halves=(both,))
    local = {}
    for s in range(1, full + 1):
        came = r, l
        r, turn = lax.optimization_barrier((r, turn))
        l, turn = lax.optimization_barrier((l, turn))
        if s < full:
            r, l = right(r), left(l)
        elif odd:
            ends = right(r[:1]), left(l[1:])
        local[s], totals, turn = expert(turn, *came, halves=(both, both), totals=totals)
    assert odd, "even ring"
    *ends, turn = lax.optimization_barrier((*ends, turn))
    local[full + 1], group, turn = expert(turn, *ends, halves=((0,), (1,)), last=True)

    def add(*terms):
        return sum(t.astype(F32) for t in terms).astype(BF16)

    def finish(*terms, rows):
        shape = lambda *s: jax.ShapeDtypeStruct(s, BF16)
        return pl.pallas_call(
            functools.partial(finish_kernel, len(terms)),
            out_shape=(shape(width // rows, ff), shape(width // rows, ff))
            + (shape(ff // rows, width), TOKEN),
            in_specs=[VMEM] * len(terms),
            out_specs=(VMEM,) * 4,
            compiler_params=PARAMS,
            name="finish",
        )(*terms)

    if groups == 2:
        mine, other, turn = weight_sums(turn, totals, group, 1)
        send = add(mine, swap(other))
        mine, other, turn = weight_sums(turn, totals, group, 0)
        got = lax.ppermute(send, "dp", [(0, 1), (1, 0)])
        terms = (mine, swap(other), got)
        grads = finish(*terms, rows=2)
    else:
        mine, other, turn = weight_sums(turn, totals, group)
        grads = finish(add(mine, swap(other)), rows=1)
        turn, grads = grads[-1], [
            lax.psum_scatter(v, "dp", scatter_dimension=0, tiled=True) for v in grads[:-1]
        ]
        grads = (*grads, turn)
    *grads, turn = grads

    def back(side, move):
        moving = None
        if odd:
            moving = move(local[full + 1][side])
        for s in range(full, 0, -1):
            here = local[s][side]
            if moving is None:
                moving = here
            else:
                if moving.shape != here.shape:
                    at = [(0, 1), (1, 0)][side]
                    moving = jnp.pad(moving, [at] + [(0, 0)] * (moving.ndim - 1))
                moving = add(moving, here)
            moving = move(moving)
        return moving

    parts = (home, back(0, left), back(1, right))
    grad_tokens, grad_probs = pl.pallas_call(
        functools.partial(home_kernel, len(parts)),
        out_shape=(
            jax.ShapeDtypeStruct((tok_dev, width), BF16),
            jax.ShapeDtypeStruct(ids_t.shape, F32),
        ),
        in_specs=[ANY] + [VMEM] * (1 + len(parts)),
        out_specs=(VMEM, VMEM),
        compiler_params=PARAMS,
        name="home",
    )(turn, ids_t, *parts)
    return (
        grad_tokens,
        grad_probs.T.astype(BF16),
        *(v[None] for v in grads),
    )


def solution(mesh):
    return jax.shard_map(
        on_device,
        mesh=mesh,
        in_specs=(
            P(("dp", "expert"), None),
            P(("dp", "expert"), None),
            P(("dp", "expert"), None),
            P(("dp", "expert"), None),
            P("expert", None, None),
            P("expert", None, None),
            P("expert", None, None),
        ),
        out_specs=(
            P(("dp", "expert"), None),
            P(("dp", "expert"), None),
            P("expert", "dp", None),
            P("expert", "dp", None),
            P("expert", "dp", None),
        ),
        check_vma=False,
    )
```

```python
import functools

import jax
import jax.numpy as jnp
from jax import lax
from jax.experimental import pallas as pl
from jax.experimental.pallas import tpu as pltpu
from jax.sharding import PartitionSpec as P

BF16, F32 = jnp.bfloat16, jnp.float32
ROWS, LANES = 16, 128
VMEM = pl.BlockSpec(memory_space=pltpu.VMEM)
ANY = pl.BlockSpec(memory_space=pl.ANY)
PIECES = 3
STEPS = 4
EXPERT_VMEM = 16 * 1024 * 1024
TOKEN = jax.ShapeDtypeStruct((8, LANES), F32)
PARAMS = pltpu.CompilerParams(vmem_limit_bytes=16 * 1024 * 1024)


def iota(shape, dim):
    return lax.broadcasted_iota(jnp.int32, shape, dim)


def kept(*shape, kind=BF16):
    return jax.ShapeDtypeStruct(shape, kind)


def put_tiles(ref, first, value):
    rows, width = value.shape
    across = width // LANES
    for i in range(rows // ROWS):
        for j in range(across):
            ref[first + i * across + j] = value[
                i * ROWS : (i + 1) * ROWS, j * LANES : (j + 1) * LANES
            ]


def take_tiles(ref, first, dst, row, rows, width):
    across = width // LANES
    for i in range(rows // ROWS):
        for j in range(across):
            dst[row + i * ROWS : row + (i + 1) * ROWS, j * LANES : (j + 1) * LANES] = ref[
                first + i * across + j
            ]


def pack_kernel(tok_ref, cot_ref, ids_ref, prob_ref, out_ref, token):
    tok_dev, width = tok_ref.shape
    half = tok_dev // 2
    block = half * width // (ROWS * LANES)
    token[...] = jnp.zeros_like(token)
    ids, prob = ids_ref[...], prob_ref[...].astype(F32)
    for i in range(out_ref.shape[1] - 2 * block):
        expert = iota((ROWS, tok_dev), 0) + i * ROWS
        dense = jnp.zeros((ROWS, tok_dev), F32)
        for k in range(ids.shape[0]):
            dense += jnp.where(ids[k : k + 1] == expert, prob[k : k + 1], 0.0)
        for n in range(2):
            out_ref[n, 2 * block + i] = dense.astype(BF16)
    for n in range(2):
        put_tiles(out_ref.at[n], 0, tok_ref[n * half : (n + 1) * half])
        put_tiles(out_ref.at[n], block, cot_ref[n * half : (n + 1) * half])


def put_strips(ref, e, at, value):
    rows, width = value.shape
    for j in range(width // LANES):
        ref[e, at + j * rows : at + (j + 1) * rows] = value[:, j * LANES : (j + 1) * LANES]


def take_strips(ref, e, at, rows, width):
    return jnp.concatenate(
        [ref[e, at + j * rows : at + (j + 1) * rows] for j in range(width // LANES)], axis=1
    )


def weights_kernel(*refs):
    out_ref = refs[6]
    for e in range(2):
        wg, wu, wd = (ref[...] for ref in refs[3 * e : 3 * e + 3])
        width, ff = wg.shape
        put_strips(out_ref, e, 0, jnp.concatenate([wg, wu], axis=1))
        put_strips(out_ref, e, 2 * ff // LANES * width, wd.T)
        put_strips(out_ref, e, 3 * ff // LANES * width, jnp.concatenate([wg.T, wu.T], axis=0))


def expert_kernel(halves, half, width, ff, start, last, *refs):
    count = len(halves)
    me = lax.axis_index("expert")
    refs = refs[1:]
    packets, refs = refs[:count], refs[count:]
    weights, refs = refs[0], refs[1:]
    if start:
        before, refs = refs[0], refs[1:]
    grads, refs = refs[:count], refs[count:]
    if not last:
        totals, refs = refs[0], refs[1:]
    token, refs = refs[0], refs[1:]
    xt_ref, outs, (x_ref, dy_ref) = refs[0], (refs[1:4], refs[4:7]), refs[7:]
    token[...] = jnp.zeros_like(token)
    block = half * width // (ROWS * LANES)
    pieces = [
        (ref.at[i], grad.at[i], which)
        for ref, grad, names in zip(packets, grads, halves)
        for i, which in enumerate(names)
    ]
    extra = packets[0].shape[1] - 2 * block
    eyes = [iota((half, LANES), 0) + n * half == iota((half, LANES), 1) for n in range(2)]
    for n, (ref, _, _) in enumerate(pieces):
        take_tiles(ref, 0, x_ref, n * half, half, width)
        take_tiles(ref, block, dy_ref, n * half, half, width)
    x, dy = x_ref[...], dy_ref[...]
    rows, by_expert = None, [[0.0] * extra for _ in pieces]
    for e in range(2):
        w_gu = take_strips(weights, e, 0, width, 2 * ff)
        w_d_t = take_strips(weights, e, 2 * ff // LANES * width, width, ff)
        w_gu_t = take_strips(weights, e, 3 * ff // LANES * width, 2 * ff, width)
        mine = [iota((ROWS, LANES), 0) + i * ROWS == me ^ e for i in range(extra)]
        probs = []
        for ref, _, which in pieces:
            row = sum(
                jnp.sum(
                    jnp.where(mine[i], ref[2 * block + i].astype(F32), 0.0), axis=0, keepdims=True
                )
                for i in range(extra)
            )
            probs.append(jnp.sum(jnp.where(eyes[which], row, 0.0), axis=1, keepdims=True))
        prob = jnp.concatenate(probs, axis=0)
        both = jnp.dot(x, w_gu, preferred_element_type=F32)
        gate, up = both[:, :ff], both[:, ff:]
        dz = jnp.dot(dy, w_d_t, preferred_element_type=F32)
        sig = jax.nn.sigmoid(gate)
        act, dact = gate * sig, sig + gate * sig * (1.0 - sig)
        hidden = (act * up).astype(BF16)
        gate_grad = jnp.sum(dz * hidden.astype(F32), axis=1, keepdims=True)
        dh = prob * dz
        d_gate = (dh * up * dact).astype(BF16)
        d_up = (dh * act).astype(BF16)
        d_both = jnp.concatenate([d_gate, d_up], axis=1)
        back = jnp.dot(d_both, w_gu_t, preferred_element_type=F32)
        rows = back if rows is None else rows + back
        for n, (_, _, which) in enumerate(pieces):
            row = jnp.sum(
                jnp.where(eyes[which], gate_grad[n * half : (n + 1) * half], 0.0),
                axis=0,
                keepdims=True,
            )
            for i in range(extra):
                by_expert[n][i] += jnp.where(mine[i], row, 0.0)
        dgu_ref, ht_ref, sc_ref = outs[e]
        dgu_ref[...] = d_both
        ht_ref[...] = hidden.T
        sc_ref[...] = (prob * dy.astype(F32)).astype(BF16)
    for n, (_, grad, _) in enumerate(pieces):
        put_tiles(grad, 0, rows[n * half : (n + 1) * half].astype(BF16))
        for i in range(extra):
            grad[block + i] = by_expert[n][i].astype(BF16)
    xt_ref[...] = x.T
    if not last:
        for e, (dgu_ref, ht_ref, sc_ref) in enumerate(outs):
            at = 0
            for a, b in ((xt_ref, dgu_ref), (ht_ref, sc_ref)):
                rows = a.shape[0]
                tile = rows // STEPS
                for step in range(STEPS):
                    new = jnp.dot(
                        a[step * tile : (step + 1) * tile], b[...], preferred_element_type=F32
                    )
                    for j in range(b.shape[1] // LANES):
                        to = pl.ds(at + j * rows + step * tile, tile)
                        strip = new[:, j * LANES : (j + 1) * LANES]
                        totals[e, to] = before[e, to] + strip if start else strip
                at += rows * b.shape[1] // LANES


def weight_kernel(steps, away, turn_ref, *refs):
    totals, xt, refs = refs[0], refs[1], refs[2:]
    groups, outs, token = (refs[:3], refs[3:6]), refs[6:8], refs[8]
    part = 0 if away is None else lax.axis_index("dp") ^ away
    token[...] = jnp.zeros_like(token)
    for e, (dgu, ht, sc) in enumerate(groups):
        to = 0
        for step in range(steps):
            at = 0
            for a, b in ((xt, dgu), (ht, sc)):
                rows, across = a.shape[0], b.shape[1] // LANES
                tile = rows // STEPS
                first = pl.multiple_of((part * steps + step) * tile, tile)
                new = jnp.dot(a[pl.ds(first, tile)], b[...], preferred_element_type=F32)
                for j in range(across):
                    strip = new[:, j * LANES : (j + 1) * LANES]
                    strip += totals[e, pl.ds(at + j * rows + first, tile)]
                    for i in range(tile // ROWS):
                        outs[e][to + i * across + j] = strip[i * ROWS : (i + 1) * ROWS].astype(
                            BF16
                        )
                at += rows * across
                to += tile // ROWS * across


def weight_sums(turn, totals, group, away=None):
    parts = 1 if away is None else 2
    tiles = totals.size // (2 * parts * ROWS * LANES)
    return pl.pallas_call(
        functools.partial(weight_kernel, STEPS // parts, away),
        out_shape=(kept(tiles, ROWS, LANES),) * 2 + (TOKEN,),
        in_specs=[ANY] + [VMEM] * (1 + len(group)),
        out_specs=(VMEM,) * 3,
        compiler_params=PARAMS,
        cost_estimate=pl.CostEstimate(
            flops=2 * totals.size * group[0].shape[1] // parts,
            bytes_accessed=16 * 2**20 // parts,
            transcendentals=0,
        ),
        name="weight_sums",
    )(turn, totals, *group)


def finish_kernel(count, whole, *refs):
    outs, token = refs[count:-1], refs[-1]
    token[...] = jnp.zeros_like(token)
    width, ff = outs[2].shape[1], outs[0].shape[1]
    tile_w, tile_d = width // STEPS, ff // STEPS
    across_w, across_d = 2 * ff // LANES, width // LANES
    each = ff // LANES
    n = 0

    def total(n):
        size = refs[count - 1].shape[0]
        terms = [ref[n] for ref in refs[:whole]]
        if whole < count:
            terms.append(refs[whole + n // size][n % size])
        return sum(t.astype(F32) for t in terms).astype(BF16)

    for step in range(outs[0].shape[0] // tile_w):
        for i in range(tile_w // ROWS):
            rows = slice(step * tile_w + i * ROWS, step * tile_w + (i + 1) * ROWS)
            for j in range(across_w):
                at = slice(j % each * LANES, (j % each + 1) * LANES)
                outs[j // each][rows, at] = total(n + j)
            n += across_w
        for i in range(tile_d // ROWS):
            rows = slice(step * tile_d + i * ROWS, step * tile_d + (i + 1) * ROWS)
            for j in range(across_d):
                outs[2][rows, j * LANES : (j + 1) * LANES] = total(n + j)
            n += across_d


def home_kernel(count, turn_ref, ids_ref, *refs):
    out_ref, prob_ref = refs[count:]
    tok_dev, width = out_ref.shape
    half = tok_dev // 2
    block = half * width // (ROWS * LANES)
    across = width // LANES
    sums = []
    for n in range(2):
        total = sum(ref[n].astype(F32) for ref in refs[:count])
        for i in range(half // ROWS):
            for j in range(across):
                out_ref[
                    n * half + i * ROWS : n * half + (i + 1) * ROWS, j * LANES : (j + 1) * LANES
                ] = total[i * across + j].astype(BF16)
        sums.append(total[block:])
    by_expert = sums[0] + sums[1]
    ids, rows = ids_ref[...], []
    for k in range(ids.shape[0]):
        row = jnp.zeros((1, tok_dev), F32)
        for i in range(by_expert.shape[0]):
            expert = iota((ROWS, tok_dev), 0) + i * ROWS
            row += jnp.sum(
                jnp.where(ids[k : k + 1] == expert, by_expert[i], 0.0), axis=0, keepdims=True
            )
        rows.append(row)
    prob_ref[...] = jnp.concatenate(rows, axis=0).astype(BF16)


def on_device(tokens, cotangent, expert_ids, gate_probs, w_gate, w_up, w_down):
    tok_dev, width = tokens.shape
    ff = w_gate.shape[2]
    half = tok_dev // 2
    devices = lax.axis_size("expert")
    groups = lax.axis_size("dp")
    experts = devices * w_gate.shape[0]
    block = half * width // (ROWS * LANES)
    extra = experts // ROWS

    chips = devices // 2
    ring = list(range(0, chips, 2)) + list(range(1, chips, 2))[::-1]
    hop = {
        d: [
            (2 * ring[i] + c, 2 * ring[(i + d) % chips] + c)
            for i in range(chips)
            for c in range(2)
        ]
        for d in (1, -1)
    }
    right = lambda v: lax.ppermute(v, "expert", hop[1])
    left = lambda v: lax.ppermute(v, "expert", hop[-1])
    swap = lambda v: lax.ppermute(v, "expert", [(i, i ^ 1) for i in range(devices)])
    full, odd = (chips - 1) // 2, chips % 2 == 0

    ids_t, probs_t = expert_ids.T, gate_probs.T
    own = (w_gate[0], w_up[0], w_down[0])

    whole = lambda v: pl.BlockSpec(v.shape, lambda i: (0,) * len(v.shape))
    packet = jax.ShapeDtypeStruct((2, 2 * block + extra, ROWS, LANES), BF16)
    start, turn = pl.pallas_call(
        pack_kernel,
        grid=(1,),
        out_shape=(packet, TOKEN),
        in_specs=[whole(v) for v in (tokens, cotangent, ids_t, probs_t)],
        out_specs=(whole(packet), whole(TOKEN)),
        compiler_params=PARAMS,
        name="pack",
    )(*(pltpu.with_memory_space_constraint(v, pltpu.HBM) for v in (tokens, cotangent, ids_t, probs_t)))

    raw = own + tuple(swap(v) for v in own)
    weights = pl.pallas_call(
        weights_kernel,
        out_shape=kept(2, 5 * ff // LANES * width, LANES),
        in_specs=[VMEM] * 6,
        out_specs=VMEM,
        compiler_params=PARAMS,
        cost_estimate=pl.CostEstimate(flops=0, bytes_accessed=24 * width * ff, transcendentals=0),
        name="weights",
    )(*raw)

    def expert(turn, *packets, halves, totals=None, last=False):
        rows = half * sum(len(h) for h in halves)
        count = len(packets)
        groups = [(width, rows)] + [(rows, 2 * ff), (ff, rows), (rows, width)] * 2
        sums = (kept(2, 3 * ff // LANES * width, LANES, kind=F32),)
        start = totals is not None and not last
        out_shape = tuple(kept(len(h), block + extra, ROWS, LANES) for h in halves)
        out_shape += () if last else sums
        out_shape += (TOKEN,)
        scratch = [(rows, width), (rows, width)]
        if last:
            out_shape += tuple(kept(*s) for s in groups)
        else:
            scratch = groups + scratch
        inputs = (turn, *packets, weights) + ((totals,) if start else ())
        outs = pl.pallas_call(
            functools.partial(expert_kernel, halves, half, width, ff, start, last),
            out_shape=out_shape,
            in_specs=[ANY] + [VMEM] * (len(inputs) - 1),
            out_specs=(VMEM,) * len(out_shape),
            scratch_shapes=[pltpu.VMEM(s, BF16) for s in scratch],

            compiler_params=pltpu.CompilerParams(vmem_limit_bytes=EXPERT_VMEM),
            cost_estimate=pl.CostEstimate(
                flops=(20 if last else 32) * rows * width * ff,
                bytes_accessed=8 * 2**20,
                transcendentals=2 * rows * ff,
            ),
            name="expert",
        )(*inputs)
        grads, outs = outs[:count], outs[count:]
        if last:
            return grads, outs[1:], outs[0]
        return grads, outs[0], outs[1]

    both = (0, 1)
    totals = None
    r, l = right(start), left(start)
    (home,), totals, turn = expert(turn, start, halves=(both,))
    local = {}
    for s in range(1, full + 1):
        came = r, l
        r, turn = lax.optimization_barrier((r, turn))
        l, turn = lax.optimization_barrier((l, turn))
        if s < full:
            r, l = right(r), left(l)
        elif odd:
            ends = right(r[:1]), left(l[1:])
        local[s], totals, turn = expert(turn, *came, halves=(both, both), totals=totals)
    assert odd, "even ring"
    *ends, turn = lax.optimization_barrier((*ends, turn))
    local[full + 1], group, turn = expert(turn, *ends, halves=((0,), (1,)), last=True)

    def add(*terms):
        return sum(t.astype(F32) for t in terms).astype(BF16)

    def finish(*terms, rows, whole):
        shape = lambda *s: jax.ShapeDtypeStruct(s, BF16)
        return pl.pallas_call(
            functools.partial(finish_kernel, len(terms), whole),
            out_shape=(shape(width // rows, ff), shape(width // rows, ff))
            + (shape(ff // rows, width), TOKEN),
            in_specs=[VMEM] * len(terms),
            out_specs=(VMEM,) * 4,
            compiler_params=PARAMS,
            name="finish",
        )(*terms)

    if groups == 2:
        mine, other, turn = weight_sums(turn, totals, group, 1)
        came = swap(other)
        size = mine.shape[0] // PIECES
        cuts = [slice(i * size, (i + 1) * size) for i in range(PIECES)]
        send = [add(mine[cut], came[cut]) for cut in cuts]
        mine, other, turn = weight_sums(turn, totals, group, 0)
        got = [lax.ppermute(v, "dp", [(0, 1), (1, 0)]) for v in send]
        for n in range(min(PIECES - 1, full)):
            at = full - 1 - n if PIECES > 2 else 1
            *local[at], got[n] = lax.optimization_barrier((*local[at], got[n]))
        grads = finish(mine, swap(other), *got, rows=2, whole=2)
    else:
        mine, other, turn = weight_sums(turn, totals, group)
        grads = finish(add(mine, swap(other)), rows=1, whole=1)
        turn, grads = grads[-1], [
            lax.psum_scatter(v, "dp", scatter_dimension=0, tiled=True) for v in grads[:-1]
        ]
        grads = (*grads, turn)
    *grads, turn = grads

    def back(side, move):
        moving = None
        if odd:
            moving = move(local[full + 1][side])
        for s in range(full, 0, -1):
            here = local[s][side]
            if moving is None:
                moving = here
            else:
                if moving.shape != here.shape:
                    at = [(0, 1), (1, 0)][side]
                    moving = jnp.pad(moving, [at] + [(0, 0)] * (moving.ndim - 1))
                moving = add(moving, here)
            moving = move(moving)
        return moving

    parts = (home, back(0, left), back(1, right))
    grad_tokens, grad_probs = pl.pallas_call(
        functools.partial(home_kernel, len(parts)),
        out_shape=(
            jax.ShapeDtypeStruct((tok_dev, width), BF16),
            jax.ShapeDtypeStruct(ids_t.shape, BF16),
        ),
        in_specs=[ANY] + [VMEM] * (1 + len(parts)),
        out_specs=(VMEM, VMEM),
        compiler_params=PARAMS,
        name="home",
    )(turn, ids_t, *parts)
    return (
        grad_tokens,
        grad_probs.T,
        *(v[None] for v in grads),
    )


def solution(mesh):
    return jax.shard_map(
        on_device,
        mesh=mesh,
        in_specs=(
            P(("dp", "expert"), None),
            P(("dp", "expert"), None),
            P(("dp", "expert"), None),
            P(("dp", "expert"), None),
            P("expert", None, None),
            P("expert", None, None),
            P("expert", None, None),
        ),
        out_specs=(
            P(("dp", "expert"), None),
            P(("dp", "expert"), None),
            P("expert", "dp", None),
            P("expert", "dp", None),
            P("expert", "dp", None),
        ),
        check_vma=False,
    )
```

```python
import functools

import jax
import jax.numpy as jnp
from jax import lax
from jax.experimental import pallas as pl
from jax.experimental.pallas import tpu as pltpu
from jax.sharding import PartitionSpec as P

BF16, F32 = jnp.bfloat16, jnp.float32
ROWS, LANES = 16, 128
VMEM = pl.BlockSpec(memory_space=pltpu.VMEM)
ANY = pl.BlockSpec(memory_space=pl.ANY)
SHARES = (1, 1, 2)
STEPS = 4
EXPERT_VMEM = 16 * 1024 * 1024
TOKEN = jax.ShapeDtypeStruct((8, LANES), F32)
PARAMS = pltpu.CompilerParams(vmem_limit_bytes=16 * 1024 * 1024)


def iota(shape, dim):
    return lax.broadcasted_iota(jnp.int32, shape, dim)


def kept(*shape, kind=BF16):
    return jax.ShapeDtypeStruct(shape, kind)


def put_tiles(ref, first, value):
    rows, width = value.shape
    across = width // LANES
    for i in range(rows // ROWS):
        for j in range(across):
            ref[first + i * across + j] = value[
                i * ROWS : (i + 1) * ROWS, j * LANES : (j + 1) * LANES
            ]


def take_tiles(ref, first, dst, row, rows, width):
    across = width // LANES
    for i in range(rows // ROWS):
        for j in range(across):
            dst[row + i * ROWS : row + (i + 1) * ROWS, j * LANES : (j + 1) * LANES] = ref[
                first + i * across + j
            ]


def pack_kernel(tok_ref, cot_ref, ids_ref, prob_ref, out_ref, token):
    tok_dev, width = tok_ref.shape
    half = tok_dev // 2
    block = half * width // (ROWS * LANES)
    token[...] = jnp.zeros_like(token)
    ids, prob = ids_ref[...], prob_ref[...].astype(F32)
    for i in range(out_ref.shape[1] - 2 * block):
        expert = iota((ROWS, tok_dev), 0) + i * ROWS
        dense = jnp.zeros((ROWS, tok_dev), F32)
        for k in range(ids.shape[0]):
            dense += jnp.where(ids[k : k + 1] == expert, prob[k : k + 1], 0.0)
        for n in range(2):
            out_ref[n, 2 * block + i] = dense.astype(BF16)
    for n in range(2):
        put_tiles(out_ref.at[n], 0, tok_ref[n * half : (n + 1) * half])
        put_tiles(out_ref.at[n], block, cot_ref[n * half : (n + 1) * half])


def put_strips(ref, e, at, value):
    rows, width = value.shape
    for j in range(width // LANES):
        ref[e, at + j * rows : at + (j + 1) * rows] = value[:, j * LANES : (j + 1) * LANES]


def take_strips(ref, e, at, rows, width):
    return jnp.concatenate(
        [ref[e, at + j * rows : at + (j + 1) * rows] for j in range(width // LANES)], axis=1
    )


def weights_kernel(*refs):
    out_ref = refs[6]
    for e in range(2):
        wg, wu, wd = (ref[...] for ref in refs[3 * e : 3 * e + 3])
        width, ff = wg.shape
        put_strips(out_ref, e, 0, jnp.concatenate([wg, wu], axis=1))
        put_strips(out_ref, e, 2 * ff // LANES * width, wd.T)
        put_strips(out_ref, e, 3 * ff // LANES * width, jnp.concatenate([wg.T, wu.T], axis=0))


def expert_kernel(halves, half, width, ff, start, last, *refs):
    count = len(halves)
    me = lax.axis_index("expert")
    refs = refs[1:]
    packets, refs = refs[:count], refs[count:]
    weights, refs = refs[0], refs[1:]
    if start:
        before, refs = refs[0], refs[1:]
    grads, refs = refs[:count], refs[count:]
    if not last:
        totals, refs = refs[0], refs[1:]
    token, refs = refs[0], refs[1:]
    xt_ref, outs, (x_ref, dy_ref) = refs[0], (refs[1:4], refs[4:7]), refs[7:]
    token[...] = jnp.zeros_like(token)
    block = half * width // (ROWS * LANES)
    pieces = [
        (ref.at[i], grad.at[i], which)
        for ref, grad, names in zip(packets, grads, halves)
        for i, which in enumerate(names)
    ]
    extra = packets[0].shape[1] - 2 * block
    eyes = [iota((half, LANES), 0) + n * half == iota((half, LANES), 1) for n in range(2)]
    for n, (ref, _, _) in enumerate(pieces):
        take_tiles(ref, 0, x_ref, n * half, half, width)
        take_tiles(ref, block, dy_ref, n * half, half, width)
    x, dy = x_ref[...], dy_ref[...]
    rows, by_expert = None, [[0.0] * extra for _ in pieces]
    for e in range(2):
        w_gu = take_strips(weights, e, 0, width, 2 * ff)
        w_d_t = take_strips(weights, e, 2 * ff // LANES * width, width, ff)
        w_gu_t = take_strips(weights, e, 3 * ff // LANES * width, 2 * ff, width)
        mine = [iota((ROWS, LANES), 0) + i * ROWS == me ^ e for i in range(extra)]
        probs = []
        for ref, _, which in pieces:
            row = sum(
                jnp.sum(
                    jnp.where(mine[i], ref[2 * block + i].astype(F32), 0.0), axis=0, keepdims=True
                )
                for i in range(extra)
            )
            probs.append(jnp.sum(jnp.where(eyes[which], row, 0.0), axis=1, keepdims=True))
        prob = jnp.concatenate(probs, axis=0)
        both = jnp.dot(x, w_gu, preferred_element_type=F32)
        gate, up = both[:, :ff], both[:, ff:]
        dz = jnp.dot(dy, w_d_t, preferred_element_type=F32)
        sig = jax.nn.sigmoid(gate)
        act, dact = gate * sig, sig + gate * sig * (1.0 - sig)
        hidden = (act * up).astype(BF16)
        gate_grad = jnp.sum(dz * hidden.astype(F32), axis=1, keepdims=True)
        dh = prob * dz
        d_gate = (dh * up * dact).astype(BF16)
        d_up = (dh * act).astype(BF16)
        d_both = jnp.concatenate([d_gate, d_up], axis=1)
        back = jnp.dot(d_both, w_gu_t, preferred_element_type=F32)
        rows = back if rows is None else rows + back
        for n, (_, _, which) in enumerate(pieces):
            row = jnp.sum(
                jnp.where(eyes[which], gate_grad[n * half : (n + 1) * half], 0.0),
                axis=0,
                keepdims=True,
            )
            for i in range(extra):
                by_expert[n][i] += jnp.where(mine[i], row, 0.0)
        dgu_ref, ht_ref, sc_ref = outs[e]
        dgu_ref[...] = d_both
        ht_ref[...] = hidden.T
        sc_ref[...] = (prob * dy.astype(F32)).astype(BF16)
    for n, (_, grad, _) in enumerate(pieces):
        put_tiles(grad, 0, rows[n * half : (n + 1) * half].astype(BF16))
        for i in range(extra):
            grad[block + i] = by_expert[n][i].astype(BF16)
    xt_ref[...] = x.T
    if not last:
        for e, (dgu_ref, ht_ref, sc_ref) in enumerate(outs):
            at = 0
            for a, b in ((xt_ref, dgu_ref), (ht_ref, sc_ref)):
                rows = a.shape[0]
                tile = rows // STEPS
                for step in range(STEPS):
                    new = jnp.dot(
                        a[step * tile : (step + 1) * tile], b[...], preferred_element_type=F32
                    )
                    for j in range(b.shape[1] // LANES):
                        to = pl.ds(at + j * rows + step * tile, tile)
                        strip = new[:, j * LANES : (j + 1) * LANES]
                        totals[e, to] = before[e, to] + strip if start else strip
                at += rows * b.shape[1] // LANES


def weight_kernel(steps, away, turn_ref, *refs):
    totals, xt, refs = refs[0], refs[1], refs[2:]
    groups, outs, token = (refs[:3], refs[3:6]), refs[6:8], refs[8]
    part = 0 if away is None else lax.axis_index("dp") ^ away
    token[...] = jnp.zeros_like(token)
    for e, (dgu, ht, sc) in enumerate(groups):
        to = 0
        for step in range(steps):
            at = 0
            for a, b in ((xt, dgu), (ht, sc)):
                rows, across = a.shape[0], b.shape[1] // LANES
                tile = rows // STEPS
                first = pl.multiple_of((part * steps + step) * tile, tile)
                new = jnp.dot(a[pl.ds(first, tile)], b[...], preferred_element_type=F32)
                for j in range(across):
                    strip = new[:, j * LANES : (j + 1) * LANES]
                    strip += totals[e, pl.ds(at + j * rows + first, tile)]
                    for i in range(tile // ROWS):
                        outs[e][to + i * across + j] = strip[i * ROWS : (i + 1) * ROWS].astype(
                            BF16
                        )
                at += rows * across
                to += tile // ROWS * across


def weight_sums(turn, totals, group, away=None):
    parts = 1 if away is None else 2
    tiles = totals.size // (2 * parts * ROWS * LANES)
    return pl.pallas_call(
        functools.partial(weight_kernel, STEPS // parts, away),
        out_shape=(kept(tiles, ROWS, LANES),) * 2 + (TOKEN,),
        in_specs=[ANY] + [VMEM] * (1 + len(group)),
        out_specs=(VMEM,) * 3,
        compiler_params=PARAMS,
        cost_estimate=pl.CostEstimate(
            flops=2 * totals.size * group[0].shape[1] // parts,
            bytes_accessed=16 * 2**20 // parts,
            transcendentals=0,
        ),
        name="weight_sums",
    )(turn, totals, *group)


def finish_kernel(count, whole, *refs):
    outs, token = refs[count:-1], refs[-1]
    token[...] = jnp.zeros_like(token)
    width, ff = outs[2].shape[1], outs[0].shape[1]
    tile_w, tile_d = width // STEPS, ff // STEPS
    across_w, across_d = 2 * ff // LANES, width // LANES
    each = ff // LANES
    n = 0

    def total(n):
        terms = [ref[n] for ref in refs[:whole]]
        for ref in refs[whole:count]:
            if 0 <= n < ref.shape[0]:
                terms.append(ref[n])
            n -= ref.shape[0]
        return sum(t.astype(F32) for t in terms).astype(BF16)

    for step in range(outs[0].shape[0] // tile_w):
        for i in range(tile_w // ROWS):
            rows = slice(step * tile_w + i * ROWS, step * tile_w + (i + 1) * ROWS)
            for j in range(across_w):
                at = slice(j % each * LANES, (j % each + 1) * LANES)
                outs[j // each][rows, at] = total(n + j)
            n += across_w
        for i in range(tile_d // ROWS):
            rows = slice(step * tile_d + i * ROWS, step * tile_d + (i + 1) * ROWS)
            for j in range(across_d):
                outs[2][rows, j * LANES : (j + 1) * LANES] = total(n + j)
            n += across_d


def home_kernel(count, turn_ref, ids_ref, *refs):
    out_ref, prob_ref = refs[count:]
    tok_dev, width = out_ref.shape
    half = tok_dev // 2
    block = half * width // (ROWS * LANES)
    across = width // LANES
    sums = []
    for n in range(2):
        total = sum(ref[n].astype(F32) for ref in refs[:count])
        for i in range(half // ROWS):
            for j in range(across):
                out_ref[
                    n * half + i * ROWS : n * half + (i + 1) * ROWS, j * LANES : (j + 1) * LANES
                ] = total[i * across + j].astype(BF16)
        sums.append(total[block:])
    by_expert = sums[0] + sums[1]
    ids, rows = ids_ref[...], []
    for k in range(ids.shape[0]):
        row = jnp.zeros((1, tok_dev), F32)
        for i in range(by_expert.shape[0]):
            expert = iota((ROWS, tok_dev), 0) + i * ROWS
            row += jnp.sum(
                jnp.where(ids[k : k + 1] == expert, by_expert[i], 0.0), axis=0, keepdims=True
            )
        rows.append(row)
    prob_ref[...] = jnp.concatenate(rows, axis=0).astype(BF16)


def last_kernel(count, whole, sides, *refs):
    inputs, outs = refs[: count + 1 + sides], refs[count + 1 + sides :]
    finish_kernel(count, whole, *inputs[:count], *outs[:4])
    home_kernel(sides, None, *inputs[count:], *outs[4:])


def on_device(tokens, cotangent, expert_ids, gate_probs, w_gate, w_up, w_down):
    tok_dev, width = tokens.shape
    ff = w_gate.shape[2]
    half = tok_dev // 2
    devices = lax.axis_size("expert")
    groups = lax.axis_size("dp")
    experts = devices * w_gate.shape[0]
    block = half * width // (ROWS * LANES)
    extra = experts // ROWS

    chips = devices // 2
    ring = list(range(0, chips, 2)) + list(range(1, chips, 2))[::-1]
    hop = {
        d: [
            (2 * ring[i] + c, 2 * ring[(i + d) % chips] + c)
            for i in range(chips)
            for c in range(2)
        ]
        for d in (1, -1)
    }
    right = lambda v: lax.ppermute(v, "expert", hop[1])
    left = lambda v: lax.ppermute(v, "expert", hop[-1])
    swap = lambda v: lax.ppermute(v, "expert", [(i, i ^ 1) for i in range(devices)])
    full, odd = (chips - 1) // 2, chips % 2 == 0

    ids_t, probs_t = expert_ids.T, gate_probs.T
    own = (w_gate[0], w_up[0], w_down[0])

    whole = lambda v: pl.BlockSpec(v.shape, lambda i: (0,) * len(v.shape))
    packet = jax.ShapeDtypeStruct((2, 2 * block + extra, ROWS, LANES), BF16)
    start, turn = pl.pallas_call(
        pack_kernel,
        grid=(1,),
        out_shape=(packet, TOKEN),
        in_specs=[whole(v) for v in (tokens, cotangent, ids_t, probs_t)],
        out_specs=(whole(packet), whole(TOKEN)),
        compiler_params=PARAMS,
        name="pack",
    )(*(pltpu.with_memory_space_constraint(v, pltpu.HBM) for v in (tokens, cotangent, ids_t, probs_t)))

    raw = own + tuple(swap(v) for v in own)
    weights = pl.pallas_call(
        weights_kernel,
        out_shape=kept(2, 5 * ff // LANES * width, LANES),
        in_specs=[VMEM] * 6,
        out_specs=VMEM,
        compiler_params=PARAMS,
        cost_estimate=pl.CostEstimate(flops=0, bytes_accessed=24 * width * ff, transcendentals=0),
        name="weights",
    )(*raw)

    def expert(turn, *packets, halves, totals=None, last=False):
        rows = half * sum(len(h) for h in halves)
        count = len(packets)
        groups = [(width, rows)] + [(rows, 2 * ff), (ff, rows), (rows, width)] * 2
        sums = (kept(2, 3 * ff // LANES * width, LANES, kind=F32),)
        start = totals is not None and not last
        out_shape = tuple(kept(len(h), block + extra, ROWS, LANES) for h in halves)
        out_shape += () if last else sums
        out_shape += (TOKEN,)
        scratch = [(rows, width), (rows, width)]
        if last:
            out_shape += tuple(kept(*s) for s in groups)
        else:
            scratch = groups + scratch
        inputs = (turn, *packets, weights) + ((totals,) if start else ())
        outs = pl.pallas_call(
            functools.partial(expert_kernel, halves, half, width, ff, start, last),
            out_shape=out_shape,
            in_specs=[ANY] + [VMEM] * (len(inputs) - 1),
            out_specs=(VMEM,) * len(out_shape),
            scratch_shapes=[pltpu.VMEM(s, BF16) for s in scratch],

            compiler_params=pltpu.CompilerParams(vmem_limit_bytes=EXPERT_VMEM),
            cost_estimate=pl.CostEstimate(
                flops=(20 if last else 32) * rows * width * ff,
                bytes_accessed=8 * 2**20,
                transcendentals=2 * rows * ff,
            ),
            name="expert",
        )(*inputs)
        grads, outs = outs[:count], outs[count:]
        if last:
            return grads, outs[1:], outs[0]
        return grads, outs[0], outs[1]

    both = (0, 1)
    totals = None
    r, l = right(start), left(start)
    (home,), totals, turn = expert(turn, start, halves=(both,))
    local = {}
    for s in range(1, full + 1):
        came = r, l
        r, turn = lax.optimization_barrier((r, turn))
        l, turn = lax.optimization_barrier((l, turn))
        if s < full:
            r, l = right(r), left(l)
        elif odd:
            ends = right(r[:1]), left(l[1:])
        local[s], totals, turn = expert(turn, *came, halves=(both, both), totals=totals)
    assert odd, "even ring"
    *ends, turn = lax.optimization_barrier((*ends, turn))
    local[full + 1], group, turn = expert(turn, *ends, halves=((0,), (1,)), last=True)

    def add(*terms):
        return sum(t.astype(F32) for t in terms).astype(BF16)

    def finish(*terms, rows, whole):
        shape = lambda *s: jax.ShapeDtypeStruct(s, BF16)
        return pl.pallas_call(
            functools.partial(finish_kernel, len(terms), whole),
            out_shape=(shape(width // rows, ff), shape(width // rows, ff))
            + (shape(ff // rows, width), TOKEN),
            in_specs=[VMEM] * len(terms),
            out_specs=(VMEM,) * 4,
            compiler_params=PARAMS,
            name="finish",
        )(*terms)

    if groups == 2:
        mine, other, turn = weight_sums(turn, totals, group, 1)
        came = swap(other)
        marks = [mine.shape[0] * sum(SHARES[:i]) // sum(SHARES) for i in range(len(SHARES) + 1)]
        cuts = [slice(*cut) for cut in zip(marks[:-1], marks[1:])]
        send = [add(mine[cut], came[cut]) for cut in cuts]
        mine, other, turn = weight_sums(turn, totals, group, 0)
        got = [lax.ppermute(v, "dp", [(0, 1), (1, 0)]) for v in send]
        for n in range(len(SHARES) - 1):
            at = full - 1 - n
            *local[at], got[n] = lax.optimization_barrier((*local[at], got[n]))
        terms = mine, swap(other), *got
    else:
        mine, other, turn = weight_sums(turn, totals, group)
        grads = finish(add(mine, swap(other)), rows=1, whole=1)
        turn, grads = grads[-1], [
            lax.psum_scatter(v, "dp", scatter_dimension=0, tiled=True) for v in grads[:-1]
        ]
        grads = (*grads, turn)
    if groups != 2:
        *grads, turn = grads

    def back(side, move):
        moving = None
        if odd:
            moving = move(local[full + 1][side])
        for s in range(full, 0, -1):
            here = local[s][side]
            if moving is None:
                moving = here
            else:
                if moving.shape != here.shape:
                    at = [(0, 1), (1, 0)][side]
                    moving = jnp.pad(moving, [at] + [(0, 0)] * (moving.ndim - 1))
                moving = add(moving, here)
            moving = move(moving)
        return moving

    parts = (home, back(0, left), back(1, right))
    if groups == 2:
        shape = lambda *s: jax.ShapeDtypeStruct(s, BF16)
        *grads, turn, grad_tokens, grad_probs = pl.pallas_call(
            functools.partial(last_kernel, len(terms), 2, len(parts)),
            out_shape=(shape(width // 2, ff), shape(width // 2, ff), shape(ff // 2, width), TOKEN)
            + (shape(tok_dev, width), shape(*ids_t.shape)),
            in_specs=[VMEM] * (len(terms) + 1 + len(parts)),
            out_specs=(VMEM,) * 6,
            compiler_params=PARAMS,
            name="last",
        )(*terms, ids_t, *parts)
    else:
        grad_tokens, grad_probs = pl.pallas_call(
            functools.partial(home_kernel, len(parts)),
            out_shape=(
                jax.ShapeDtypeStruct((tok_dev, width), BF16),
                jax.ShapeDtypeStruct(ids_t.shape, BF16),
            ),
            in_specs=[ANY] + [VMEM] * (1 + len(parts)),
            out_specs=(VMEM, VMEM),
            compiler_params=PARAMS,
            name="home",
        )(turn, ids_t, *parts)
    return (
        grad_tokens,
        grad_probs.T,
        *(v[None] for v in grads),
    )


def solution(mesh):
    return jax.shard_map(
        on_device,
        mesh=mesh,
        in_specs=(
            P(("dp", "expert"), None),
            P(("dp", "expert"), None),
            P(("dp", "expert"), None),
            P(("dp", "expert"), None),
            P("expert", None, None),
            P("expert", None, None),
            P("expert", None, None),
        ),
        out_specs=(
            P(("dp", "expert"), None),
            P(("dp", "expert"), None),
            P("expert", "dp", None),
            P("expert", "dp", None),
            P("expert", "dp", None),
        ),
        check_vma=False,
    )
```
